256 devices in a mesh: row: 8 (over x, core), col: 32 (over y, z).
Axes of the slice: x: 4, y: 4, z: 8, core: 2. Of those that a mesh axis runs over, the one named last changes fastest.
Arguments:
- tokens: bfloat16 [1024, 8192], P('col', 'row'), may hold values from -6 to 6
- gate_weight: bfloat16 [8192, 16384], P('row', 'col'), may hold values from -0.0625 to 0.0625
- up_weight: bfloat16 [8192, 16384], P('row', 'col'), may hold values from -0.0625 to 0.0625
- down_weight: bfloat16 [16384, 8192], P('col', 'row'), may hold values from -0.046875 to 0.046875
- out_grad: bfloat16 [1024, 8192], P('col', 'row'), may hold values from -1.5 to 1.5
Outputs:
- layer_output: bfloat16 [1024, 8192], P('col', 'row')
- input_grad: bfloat16 [1024, 8192], P('col', 'row')
- gate_weight_grad: float32 [8192, 16384], P('row', 'col')
- up_weight_grad: float32 [8192, 16384], P('row', 'col')
- down_weight_grad: float32 [16384, 8192], P('col', 'row')
The draws below stay inside these ranges and needn't reach their ends.
All inputs are finite; a program needn't handle non-finite values.
Results may differ from the reference program's by a relative error of at most 0.022.
Values may be sent and summed in bfloat16 or wider, within the bound.
No kernel may reach another device: no remote copies, remote signals or barrier semaphores. Data moves between devices by JAX's collectives and lax.ppermute only.
A program may use at most 64 MiB of HBM per device.

```python
import jax
import jax.numpy as jnp
from jax import lax

D = 8192
FF = 16384
TOKENS = 1024


def shard_levels(rng, extent, pieces, smallest, high):
    gain = 1.0
    for dim, parts in pieces:
        draws = jax.random.uniform(jax.random.fold_in(jax.random.fold_in(rng, 6), dim), (parts,), jnp.float32, smallest / len(pieces), high / len(pieces))
        gain = gain * jnp.repeat(jnp.exp(draws), extent[dim] // parts).reshape((-1,) + (1,) * (len(extent) - 1 - dim))
    return gain


def normal_values(rng, extent, width, limit, pieces=(), dtype=jnp.bfloat16):
    factor_of = shard_levels(rng, extent, pieces, -0.22, 0.18) if pieces else 1.0
    result = jax.random.normal(rng, extent, jnp.float32) * width * factor_of
    return jnp.minimum(jnp.maximum(result, -limit), limit).astype(dtype)


def setup_inputs(seed: int = 0) -> dict:
    keys = jax.random.split(jax.random.key(seed), 6)
    tokens = normal_values(keys[0], (TOKENS, D), 1.0, 6.0, ((0, 32), (1, 8)))
    gate_weight = normal_values(keys[1], (D, FF), D ** -0.5, 0.0625, ((0, 8), (1, 32)))
    up_weight = normal_values(keys[2], (D, FF), D ** -0.5, 0.0625, ((0, 8), (1, 32)))
    down_weight = normal_values(keys[3], (FF, D), FF ** -0.5, 0.046875, ((0, 32), (1, 8)))
    out_grad = normal_values(keys[4], (TOKENS, D), 0.25, 1.5, ((0, 32), (1, 8)))
    return dict(tokens=tokens, gate_weight=gate_weight, up_weight=up_weight, down_weight=down_weight, out_grad=out_grad)


def product(left_side, right_side):
    return jnp.dot(left_side, right_side, preferred_element_type=jnp.float32)


def product_right_t(left_side, right_side):
    return lax.dot_general(left_side, right_side, (((1,), (1,)), ((), ())), preferred_element_type=jnp.float32)


def product_left_t(left_side, right_side):
    return lax.dot_general(left_side, right_side, (((0,), (0,)), ((), ())), preferred_element_type=jnp.float32)


def reference(tokens, gate_weight, up_weight, down_weight, out_grad):
    gate_value = product(tokens, gate_weight)
    up_value = product(tokens, up_weight)
    sigmoid_gate = jax.nn.sigmoid(gate_value)
    silu_gate = gate_value * sigmoid_gate
    hidden = (silu_gate * up_value).astype(jnp.bfloat16)
    layer_output = product(hidden, down_weight).astype(jnp.bfloat16)
    hidden_grad = product_right_t(out_grad, down_weight)
    gate_grad = (hidden_grad * up_value * sigmoid_gate * (1.0 + gate_value * (1.0 - sigmoid_gate))).astype(jnp.bfloat16)
    up_grad = (hidden_grad * silu_gate).astype(jnp.bfloat16)
    input_grad = (product_right_t(gate_grad, gate_weight) + product_right_t(up_grad, up_weight)).astype(jnp.bfloat16)
    gate_weight_grad = product_left_t(tokens, gate_grad)
    up_weight_grad = product_left_t(tokens, up_grad)
    down_weight_grad = product_left_t(hidden, out_grad)
    return (layer_output, input_grad, gate_weight_grad, up_weight_grad, down_weight_grad)
```

```python
import jax
import jax.numpy as jnp
from jax import lax
from jax.sharding import Mesh, PartitionSpec as P

BF = jnp.bfloat16
F32 = jnp.float32
X, CORE, Y, Z = 4, 2, 4, 8


def product(left_side, right_side):
    return jnp.dot(left_side, right_side, preferred_element_type=F32)


def product_right_t(left_side, right_side):
    return lax.dot_general(left_side, right_side, (((1,), (1,)), ((), ())), preferred_element_type=F32)


def product_left_t(left_side, right_side):
    return lax.dot_general(left_side, right_side, (((0,), (0,)), ((), ())), preferred_element_type=F32)


def shift(block, axis, size, step):
    return lax.ppermute(block, axis, [(i, (i + step) % size) for i in range(size)])


def exchange(blocks, axis):
    return lax.all_to_all(blocks, axis, split_axis=0, concat_axis=0, tiled=True)


def gather_z(block):
    rows, width = block.shape
    copies = jnp.broadcast_to(block[None], (Z, rows, width)).reshape(Z * rows, width)
    return exchange(copies, "z")


def gather_y(block):
    return [block, shift(block, "y", Y, 1), shift(block, "y", Y, 3), shift(block, "y", Y, 2)]


def gather_col(block):
    own, one, three, two = gather_y(gather_z(block))
    return jnp.concatenate([own, one, two, three], axis=0)


def sum_parts(parts, count):
    rows = parts.shape[0] // count
    return jnp.sum(parts.reshape((count, rows) + parts.shape[1:]).astype(F32), axis=0)


def reduce_row(partial):
    pair = sum_parts(exchange(partial, "core"), CORE).astype(BF)
    return sum_parts(exchange(pair, "x"), X)


def gather_row(share):
    return lax.all_gather(lax.all_gather(share, "x", axis=0, tiled=True), "core", axis=0, tiled=True)


def reduce_col(partial):
    rows = partial.shape[0] // Y
    pieces = [partial[j * rows : (j + 1) * rows] for j in range(Y)]
    total = (
        pieces[0].astype(F32)
        + shift(pieces[1], "y", Y, 3).astype(F32)
        + shift(pieces[3], "y", Y, 1).astype(F32)
        + shift(pieces[2], "y", Y, 2).astype(F32)
    ).astype(BF)
    return sum_parts(exchange(total, "z"), Z).astype(BF)


def body(tokens, gate_weight, up_weight, down_weight, out_grad):
    width = gate_weight.shape[1]
    all_tokens = gather_col(tokens)
    all_grads = gather_col(out_grad)
    partial = jnp.concatenate(
        [product(all_tokens, gate_weight).astype(BF), product(all_tokens, up_weight).astype(BF)], axis=1
    )
    gate_up = reduce_row(partial)
    gate_value = gate_up[:, :width]
    up_value = gate_up[:, width:]
    sigmoid_gate = jax.nn.sigmoid(gate_value)
    silu_gate = gate_value * sigmoid_gate
    hidden = gather_row((silu_gate * up_value).astype(BF))
    layer_output = reduce_col(product(hidden, down_weight).astype(BF))

    hidden_grad = reduce_row(product_right_t(all_grads, down_weight).astype(BF))
    gate_grad = (hidden_grad * up_value * sigmoid_gate * (1.0 + gate_value * (1.0 - sigmoid_gate))).astype(BF)
    up_grad = (hidden_grad * silu_gate).astype(BF)
    both = gather_row(jnp.concatenate([gate_grad, up_grad], axis=1))
    gate_grads = both[:, :width]
    up_grads = both[:, width:]
    input_partial = product_right_t(gate_grads, gate_weight) + product_right_t(up_grads, up_weight)
    input_grad = reduce_col(input_partial.astype(BF))
    gate_weight_grad = product_left_t(all_tokens, gate_grads)
    up_weight_grad = product_left_t(all_tokens, up_grads)
    down_weight_grad = product_left_t(hidden, all_grads)
    return (layer_output, input_grad, gate_weight_grad, up_weight_grad, down_weight_grad)


def solution(mesh):
    grid = Mesh(mesh.devices.reshape(X, CORE, Y, Z), ("x", "core", "y", "z"))
    row, col = ("x", "core"), ("y", "z")
    in_specs = (P(col, row), P(row, col), P(row, col), P(col, row), P(col, row))
    out_specs = (P(col, row), P(col, row), P(row, col), P(row, col), P(col, row))
    return jax.shard_map(body, mesh=grid, in_specs=in_specs, out_specs=out_specs, check_vma=False)
```

```python
import jax
import jax.numpy as jnp
from jax import lax
from jax.sharding import Mesh, PartitionSpec as P

BF = jnp.bfloat16
F32 = jnp.float32
X, CORE, Y, Z = 4, 2, 4, 8


def product(left_side, right_side):
    return jnp.dot(left_side, right_side, preferred_element_type=F32)


def product_right_t(left_side, right_side):
    return lax.dot_general(left_side, right_side, (((1,), (1,)), ((), ())), preferred_element_type=F32)


def product_left_t(left_side, right_side):
    return lax.dot_general(left_side, right_side, (((0,), (0,)), ((), ())), preferred_element_type=F32)


def shift(block, axis, step):
    size = lax.axis_size(axis)
    return lax.ppermute(block, axis, [(i, (i + step) % size) for i in range(size)])


def exchange(blocks, axis):
    return lax.all_to_all(blocks, axis, split_axis=0, concat_axis=0, tiled=True)


def gather(block, axis):
    count = lax.axis_size(axis)
    rows, width = block.shape
    copies = jnp.broadcast_to(block[None], (count, rows, width)).reshape(count * rows, width)
    return exchange(copies, axis)


def after(block, *earlier):
    return lax.optimization_barrier((block,) + earlier)[0]


def gather_y(own):
    near = [shift(own, "y", 1), shift(own, "y", 3)]
    return jnp.concatenate([own, near[0], shift(own, "y", 2), near[1]], axis=0)


def gather_y_later(own):
    pieces = lax.all_gather(own, "y", axis=0, tiled=False)
    place = lax.axis_index("y") + Y
    return jnp.concatenate(
        [lax.dynamic_index_in_dim(pieces, lax.bitwise_and(place - j, Y - 1), axis=0, keepdims=False) for j in range(Y)], axis=0
    )


def swap_core(low, high):
    first = lax.axis_index("core") == 0
    return jnp.where(first, low, high), shift(jnp.where(first, high, low), "core", 1)


def sum_parts(parts, count):
    rows = parts.shape[0] // count
    return jnp.sum(parts.reshape((count, rows) + parts.shape[1:]).astype(F32), axis=0)


def reduce_core(partial):
    rows = partial.shape[0] // CORE
    kept, received = swap_core(partial[:rows], partial[rows:])
    return (kept.astype(F32) + received.astype(F32)).astype(BF)


def reduce_x(partial):
    return sum_parts(exchange(partial, "x"), X)


def gather_core(half):
    other = shift(half, "core", 1)
    first = lax.axis_index("core") == 0
    return jnp.concatenate([jnp.where(first, half, other), jnp.where(first, other, half)], axis=0)


def reduce_col(partial):
    rows = partial.shape[0] // Y
    pieces = [partial[j * rows : (j + 1) * rows] for j in range(Y)]
    moved = [shift(pieces[1], "y", 3), shift(pieces[3], "y", 1), shift(pieces[2], "y", 2)]
    total = pieces[0].astype(F32) + moved[0].astype(F32) + moved[1].astype(F32) + moved[2].astype(F32)
    return sum_parts(exchange(total.astype(BF), "z"), Z).astype(BF)


def body(tokens, gate_weight, up_weight, down_weight, out_grad):
    width = gate_weight.shape[1]
    both_weights = jnp.concatenate([gate_weight, up_weight], axis=1)
    tokens_z = gather(tokens, "z")
    all_tokens = gather_y(tokens_z)
    grads_z = gather(after(out_grad, tokens_z), "z")
    all_grads = gather_y_later(grads_z)
    gate_up = reduce_x(reduce_core(product(all_tokens, both_weights).astype(BF)))
    gate_value = gate_up[:, :width]
    up_value = gate_up[:, width:]
    sigmoid_gate = jax.nn.sigmoid(gate_value)
    silu_gate = gate_value * sigmoid_gate
    hidden_half = gather((silu_gate * up_value).astype(BF), "x")
    hidden = gather_core(hidden_half)
    output_partial = product(hidden, down_weight).astype(BF)
    layer_output = reduce_col(output_partial)

    hidden_partial = reduce_core(product_right_t(all_grads, down_weight).astype(BF))
    hidden_grad = reduce_x(after(hidden_partial, hidden_half))
    gate_grad = (hidden_grad * up_value * sigmoid_gate * (1.0 + gate_value * (1.0 - sigmoid_gate))).astype(BF)
    up_grad = (hidden_grad * silu_gate).astype(BF)
    both_share = after(jnp.concatenate([gate_grad, up_grad], axis=1), output_partial)
    both_grads = gather_core(gather(both_share, "x"))
    input_grad = reduce_col(product_right_t(both_grads, both_weights).astype(BF))
    gate_weight_grad = product_left_t(all_tokens, both_grads[:, :width])
    up_weight_grad = product_left_t(all_tokens, both_grads[:, width:])
    down_weight_grad = product_left_t(hidden, all_grads)
    return (layer_output, input_grad, gate_weight_grad, up_weight_grad, down_weight_grad)


def solution(mesh):
    grid = Mesh(mesh.devices.reshape(X, CORE, Y, Z), ("x", "core", "y", "z"))
    row, col = ("x", "core"), ("y", "z")
    in_specs = (P(col, row), P(row, col), P(row, col), P(col, row), P(col, row))
    out_specs = (P(col, row), P(col, row), P(row, col), P(row, col), P(col, row))
    return jax.shard_map(body, mesh=grid, in_specs=in_specs, out_specs=out_specs, check_vma=False)
```

```python
import jax
import jax.numpy as jnp
from jax import lax
from jax.sharding import Mesh, PartitionSpec as P

BF = jnp.bfloat16
F32 = jnp.float32
X, CORE, Y, Z = 4, 2, 4, 8


def product(left_side, right_side):
    return jnp.dot(left_side, right_side, preferred_element_type=F32)


def product_right_t(left_side, right_side):
    return lax.dot_general(left_side, right_side, (((1,), (1,)), ((), ())), preferred_element_type=F32)


def product_left_t(left_side, right_side):
    return lax.dot_general(left_side, right_side, (((0,), (0,)), ((), ())), preferred_element_type=F32)


def shift(block, axis, step):
    size = lax.axis_size(axis)
    return lax.ppermute(block, axis, [(i, (i + step) % size) for i in range(size)])


def exchange(blocks, axis):
    return lax.all_to_all(blocks, axis, split_axis=0, concat_axis=0, tiled=True)


def gather(block, axis):
    count = lax.axis_size(axis)
    rows, width = block.shape
    copies = jnp.broadcast_to(block[None], (count, rows, width)).reshape(count * rows, width)
    return exchange(copies, axis)


def after(block, *earlier):
    return lax.optimization_barrier((block,) + earlier)[0]


def gather_y(own):
    rows = own.shape[0] // 2
    from_left, from_right = shift(own, "y", 1), shift(own, "y", 3)
    far = [shift(from_left[:rows], "y", 1), shift(from_right[rows:], "y", 3)]
    return jnp.concatenate([own, from_left] + far + [from_right], axis=0)


def gather_y_later(own):
    pieces = lax.all_gather(own, "y", axis=0, tiled=False)
    place = lax.axis_index("y") + Y
    return jnp.concatenate(
        [lax.dynamic_index_in_dim(pieces, lax.bitwise_and(place - j, Y - 1), axis=0, keepdims=False) for j in range(Y)], axis=0
    )


def swap_core(low, high):
    first = lax.axis_index("core") == 0
    return jnp.where(first, low, high), shift(jnp.where(first, high, low), "core", 1)


def sum_parts(parts, count):
    rows = parts.shape[0] // count
    return jnp.sum(parts.reshape((count, rows) + parts.shape[1:]).astype(F32), axis=0)


def reduce_core(partial):
    rows = partial.shape[0] // CORE
    kept, received = swap_core(partial[:rows], partial[rows:])
    return (kept.astype(F32) + received.astype(F32)).astype(BF)


def reduce_x(partial):
    return sum_parts(exchange(partial, "x"), X)


def gather_core(half):
    other = shift(half, "core", 1)
    first = lax.axis_index("core") == 0
    return jnp.concatenate([jnp.where(first, half, other), jnp.where(first, other, half)], axis=0)


def add(left_side, right_side):
    return (left_side.astype(F32) + right_side.astype(F32)).astype(BF)


def split_y(partial):
    rows = partial.shape[0] // Y
    return [partial[j * rows : (j + 1) * rows] for j in range(Y)]


def reduce_y_far(pieces):
    rows = pieces[2].shape[0] // 2
    return shift(pieces[2][:rows], "y", 1), shift(pieces[2][rows:], "y", 3)


def reduce_y_near(pieces, from_left, from_right):
    rows = pieces[2].shape[0] // 2
    to_right = jnp.concatenate([add(pieces[3][:rows], from_left), pieces[3][rows:]], axis=0)
    to_left = jnp.concatenate([pieces[1][:rows], add(pieces[1][rows:], from_right)], axis=0)
    return shift(to_right, "y", 1), shift(to_left, "y", 3)


def sum_y(own, from_left, from_right):
    return (own.astype(F32) + from_left.astype(F32) + from_right.astype(F32)).astype(BF)


def reduce_z(total):
    return sum_parts(exchange(total, "z"), Z).astype(BF)


def body(tokens, gate_weight, up_weight, down_weight, out_grad):
    width = gate_weight.shape[1]
    both_weights = jnp.concatenate([gate_weight, up_weight], axis=1)
    tokens_z = gather(tokens, "z")
    all_tokens = gather_y(tokens_z)
    grads_z = gather(after(out_grad, tokens_z), "z")
    all_grads = gather_y_later(grads_z)

    gate_up = reduce_x(reduce_core(product(all_tokens, both_weights).astype(BF)))
    gate_value = gate_up[:, :width]
    up_value = gate_up[:, width:]
    sigmoid_gate = jax.nn.sigmoid(gate_value)
    silu_gate = gate_value * sigmoid_gate
    hidden_share = (silu_gate * up_value).astype(BF)

    hidden_partial = reduce_core(product_right_t(all_grads, down_weight).astype(BF))
    rows = hidden_share.shape[0]
    mixed = jnp.concatenate(
        [jnp.broadcast_to(hidden_share[None], (X, rows, width)), hidden_partial.reshape(X, rows, width)], axis=1
    )
    mixed = exchange(mixed.reshape(2 * X * rows, width), "x").reshape(X, 2 * rows, width)
    hidden = gather_core(mixed[:, :rows].reshape(X * rows, width))
    hidden_grad = jnp.sum(mixed[:, rows:].astype(F32), axis=0)

    output_pieces = split_y(product(hidden, down_weight).astype(BF))
    output_far = reduce_y_far(output_pieces)
    output_near = reduce_y_near(output_pieces, *output_far)

    gate_grad = (hidden_grad * up_value * sigmoid_gate * (1.0 + gate_value * (1.0 - sigmoid_gate))).astype(BF)
    up_grad = (hidden_grad * silu_gate).astype(BF)
    both_half = after(gather(jnp.concatenate([gate_grad, up_grad], axis=1), "x"), *output_far)
    both_grads = after(gather_core(both_half), *output_near)

    input_pieces = split_y(product_right_t(both_grads, both_weights).astype(BF))
    input_near = reduce_y_near(input_pieces, *reduce_y_far(input_pieces))
    layer_output = reduce_z(sum_y(output_pieces[0], *output_near))
    gate_weight_grad = product_left_t(all_tokens, both_grads[:, :width])
    up_weight_grad = product_left_t(all_tokens, both_grads[:, width:])
    down_weight_grad = product_left_t(hidden, all_grads)
    weight_grads = (gate_weight_grad, up_weight_grad, down_weight_grad)
    input_total, weight_grads = lax.optimization_barrier((sum_y(input_pieces[0], *input_near), weight_grads))
    return (layer_output, reduce_z(input_total)) + weight_grads


def solution(mesh):
    grid = Mesh(mesh.devices.reshape(X, CORE, Y, Z), ("x", "core", "y", "z"))
    row, col = ("x", "core"), ("y", "z")
    in_specs = (P(col, row), P(row, col), P(row, col), P(col, row), P(col, row))
    out_specs = (P(col, row), P(col, row), P(row, col), P(row, col), P(col, row))
    return jax.shard_map(body, mesh=grid, in_specs=in_specs, out_specs=out_specs, check_vma=False)
```

```python
import jax
import jax.numpy as jnp
from jax import lax
from jax.sharding import Mesh, PartitionSpec as P

BF = jnp.bfloat16
F32 = jnp.float32
X, CORE, Y, Z = 4, 2, 4, 8


def product(left_side, right_side):
    return jnp.dot(left_side, right_side, preferred_element_type=F32)


def product_right_t(left_side, right_side):
    return lax.dot_general(left_side, right_side, (((1,), (1,)), ((), ())), preferred_element_type=F32)


def product_left_t(left_side, right_side):
    return lax.dot_general(left_side, right_side, (((0,), (0,)), ((), ())), preferred_element_type=F32)


def shift(block, axis, step):
    size = lax.axis_size(axis)
    return lax.ppermute(block, axis, [(i, (i + step) % size) for i in range(size)])


def exchange(blocks, axis):
    return lax.all_to_all(blocks, axis, split_axis=0, concat_axis=0, tiled=True)


def gather(block, axis):
    count = lax.axis_size(axis)
    rows, width = block.shape
    copies = jnp.broadcast_to(block[None], (count, rows, width)).reshape(count * rows, width)
    return exchange(copies, axis)


def after(block, *earlier):
    return lax.optimization_barrier((block,) + earlier)[0]


def gather_y(own):
    near = [shift(own, "y", 1), shift(own, "y", 3)]
    return [own, near[0], shift(own, "y", 2), near[1]]


def other_core(block):
    return shift(block, "core", 1)


def sum_parts(parts, count):
    rows = parts.shape[0] // count
    return jnp.sum(parts.reshape((count, rows) + parts.shape[1:]).astype(F32), axis=0)


def reduce_x(partial):
    return sum_parts(exchange(partial, "x"), X)


def split_y(partial):
    rows = partial.shape[0] // Y
    return [partial[j * rows : (j + 1) * rows] for j in range(Y)]


def move_y(pieces):
    return [shift(pieces[1], "y", 3), shift(pieces[3], "y", 1), shift(pieces[2], "y", 2)]


def sum_y(own, moved):
    total = own.astype(F32)
    for piece in moved:
        total = total + piece.astype(F32)
    return total.astype(BF)


def reduce_z(total):
    return sum_parts(exchange(total, "z"), Z).astype(BF)


def own_rows(blocks, first):
    rows = blocks[0].shape[0] // CORE
    kept = [jnp.where(first, block[:rows], block[rows:]) for block in blocks]
    sent = [jnp.where(first, block[rows:], block[:rows]) for block in blocks]
    received = other_core(jnp.concatenate(sent, axis=0)).reshape((len(blocks), rows, -1))
    return [jnp.concatenate([kept[i], received[i]], axis=1) for i in range(len(blocks))]


def own_columns(blocks, first):
    columns = blocks[0].shape[1] // CORE
    received = other_core(jnp.stack([block[:, columns:] for block in blocks]))
    return [
        jnp.where(
            first,
            jnp.concatenate([block[:, :columns], received[i]], axis=0),
            jnp.concatenate([received[i], block[:, :columns]], axis=0),
        )
        for i, block in enumerate(blocks)
    ]


def both_halves(half):
    return jnp.concatenate([half, other_core(half)], axis=0)


def body(tokens, gate_weight, up_weight, down_weight, out_grad):
    width = gate_weight.shape[1]
    features = gate_weight.shape[0]
    first = lax.axis_index("core") == 0

    own_tokens, own_grads = own_rows((tokens, out_grad), first)
    tokens_z, grads_y = lax.optimization_barrier((gather(own_tokens, "z"), jnp.stack(gather_y(own_grads))))
    tokens_half = jnp.concatenate(gather_y(tokens_z), axis=0)
    grads_half = lax.all_gather(grads_y, "z", axis=0, tiled=False)
    grads_half = jnp.swapaxes(grads_half, 0, 1).reshape(tokens_half.shape)
    both_weights = jnp.concatenate([gate_weight, up_weight], axis=1)
    both_weights = jnp.concatenate([both_weights, other_core(both_weights)], axis=0)
    down_weights = jnp.concatenate([down_weight, other_core(down_weight)], axis=1)

    def all_rows(half):
        return jnp.concatenate([half[:, :features], other_core(half[:, features:])], axis=0)

    gate_up_partial = product(tokens_half, both_weights).astype(BF)
    gate_up = sum_parts(exchange(gate_up_partial, "x"), X)
    gate_up, all_tokens = lax.optimization_barrier((gate_up, all_rows(after(tokens_half, gate_up_partial))))
    gate_value = gate_up[:, :width]
    up_value = gate_up[:, width:]
    sigmoid_gate = jax.nn.sigmoid(gate_value)
    silu_gate = gate_value * sigmoid_gate
    hidden_share = (silu_gate * up_value).astype(BF)

    hidden_partial = product_right_t(grads_half, down_weights).astype(BF)
    rows = hidden_share.shape[0]
    mixed = jnp.concatenate(
        [jnp.broadcast_to(hidden_share[None], (X, rows, width)), hidden_partial.reshape(X, rows, width)], axis=1
    )
    mixed = exchange(mixed.reshape(2 * X * rows, width), "x").reshape(X, 2 * rows, width)
    hidden_half = mixed[:, :rows].reshape(X * rows, width)
    hidden_grad = jnp.sum(mixed[:, rows:].astype(F32), axis=0)
    hidden_grad, all_out_grads = lax.optimization_barrier((hidden_grad, all_rows(grads_half)))

    output_pieces = split_y(product(hidden_half, down_weights).astype(BF))
    output_moved = move_y(output_pieces)

    gate_grad = (hidden_grad * up_value * sigmoid_gate * (1.0 + gate_value * (1.0 - sigmoid_gate))).astype(BF)
    up_grad = (hidden_grad * silu_gate).astype(BF)
    grads_both = gather(jnp.concatenate([gate_grad, up_grad], axis=1), "x")
    down_weight_grad = product_left_t(both_halves(hidden_half), all_out_grads)
    grads_both, down_weight_grad, *output_moved = lax.optimization_barrier(
        (grads_both, down_weight_grad, *output_moved)
    )
    input_pieces = split_y(product_right_t(grads_both, both_weights).astype(BF))
    input_moved = move_y(input_pieces)
    all_grads = both_halves(after(grads_both, *input_pieces))
    output_total = reduce_z(after(sum_y(output_pieces[0], output_moved), all_grads))
    gate_weight_grad = product_left_t(all_tokens, all_grads[:, :width])
    up_weight_grad = product_left_t(all_tokens, all_grads[:, width:])
    earlier = lax.optimization_barrier((output_total, gate_weight_grad, up_weight_grad))
    input_total, *earlier = lax.optimization_barrier((sum_y(input_pieces[0], input_moved), *earlier))
    layer_output, input_grad = own_columns((earlier[0], reduce_z(input_total)), first)
    return (layer_output, input_grad, earlier[1], earlier[2], down_weight_grad)


def solution(mesh):
    grid = Mesh(mesh.devices.reshape(X, CORE, Y, Z), ("x", "core", "y", "z"))
    row, col = ("x", "core"), ("y", "z")
    in_specs = (P(col, row), P(row, col), P(row, col), P(col, row), P(col, row))
    out_specs = (P(col, row), P(col, row), P(row, col), P(row, col), P(col, row))
    return jax.shard_map(body, mesh=grid, in_specs=in_specs, out_specs=out_specs, check_vma=False)
```

```python
import jax
import jax.numpy as jnp
from jax import lax
from jax.sharding import Mesh, PartitionSpec as P

BF = jnp.bfloat16
F32 = jnp.float32
X, CORE, Y, Z = 4, 2, 4, 8


def product(left_side, right_side):
    return jnp.dot(left_side, right_side, preferred_element_type=F32)


def product_right_t(left_side, right_side):
    return lax.dot_general(left_side, right_side, (((1,), (1,)), ((), ())), preferred_element_type=F32)


def product_left_t(left_side, right_side):
    return lax.dot_general(left_side, right_side, (((0,), (0,)), ((), ())), preferred_element_type=F32)


def shift(block, axis, step):
    size = lax.axis_size(axis)
    return lax.ppermute(block, axis, [(i, (i + step) % size) for i in range(size)])


def exchange(blocks, axis):
    return lax.all_to_all(blocks, axis, split_axis=0, concat_axis=0, tiled=True)


def gather(block, axis):
    count = lax.axis_size(axis)
    rows, width = block.shape
    copies = jnp.broadcast_to(block[None], (count, rows, width)).reshape(count * rows, width)
    return exchange(copies, axis)


def after(block, *earlier):
    return lax.optimization_barrier((block,) + earlier)[0]


def gather_y(own):
    near = [shift(own, "y", 1), shift(own, "y", 3)]
    return [own, near[0], shift(own, "y", 2), near[1]]


def other_core(block):
    return shift(block, "core", 1)


def sum_parts(parts, count):
    rows = parts.shape[0] // count
    return jnp.sum(parts.reshape((count, rows) + parts.shape[1:]).astype(F32), axis=0)


def reduce_x(partial):
    return sum_parts(exchange(partial, "x"), X)


def split_y(partial):
    rows = partial.shape[0] // Y
    return [partial[j * rows : (j + 1) * rows] for j in range(Y)]


def move_y(pieces):
    return [shift(pieces[1], "y", 3), shift(pieces[3], "y", 1), shift(pieces[2], "y", 2)]


def sum_y(own, moved):
    total = own.astype(F32)
    for piece in moved:
        total = total + piece.astype(F32)
    return total.astype(BF)


def reduce_z(total):
    return sum_parts(exchange(total, "z"), Z).astype(BF)


def swap_rows(blocks, first):
    rows = blocks[0].shape[0] // CORE
    kept = [jnp.where(first, block[:rows], block[rows:]) for block in blocks]
    sent = [jnp.where(first, block[rows:], block[:rows]) for block in blocks]
    received = other_core(jnp.concatenate(sent, axis=0))
    return kept, received


def own_columns(blocks, first):
    columns = blocks[0].shape[1] // CORE
    received = other_core(jnp.stack([block[:, columns:] for block in blocks]))
    return [
        jnp.where(
            first,
            jnp.concatenate([block[:, :columns], received[i]], axis=0),
            jnp.concatenate([received[i], block[:, :columns]], axis=0),
        )
        for i, block in enumerate(blocks)
    ]


def swap_rows(blocks, first):
    rows = blocks[0].shape[0] // CORE
    kept = [jnp.where(first, block[:rows], block[rows:]) for block in blocks]
    sent = [jnp.where(first, block[rows:], block[:rows]) for block in blocks]
    received = other_core(jnp.concatenate(sent, axis=0))
    return kept, received


def own_columns(blocks, first):
    columns = blocks[0].shape[1] // CORE
    received = other_core(jnp.stack([block[:, columns:] for block in blocks]))
    return [
        jnp.where(
            first,
            jnp.concatenate([block[:, :columns], received[i]], axis=0),
            jnp.concatenate([received[i], block[:, :columns]], axis=0),
        )
        for i, block in enumerate(blocks)
    ]


def both_halves(half):
    return jnp.concatenate([half, other_core(half)], axis=0)


def body(tokens, gate_weight, up_weight, down_weight, out_grad):
    width = gate_weight.shape[1]
    first = lax.axis_index("core") == 0

    (tokens_own, grads_own), received = swap_rows((tokens, out_grad), first)
    rows = tokens_own.shape[0]
    tokens_z = gather(tokens_own, "z")
    received = jnp.stack(gather_y(received))
    tokens_z, received = lax.optimization_barrier((tokens_z, received))

    def gather_z_last(block):
        whole = lax.all_gather(block, "z", axis=0, tiled=False)
        return jnp.swapaxes(whole, 0, 1).reshape(Y * Z * rows, -1)

    tokens_far = gather_z_last(received[:, :rows])
    grads_far = gather_z_last(received[:, rows:])
    grads_z = gather(after(grads_own, tokens_z), "z")
    tokens_near = jnp.concatenate(gather_y(tokens_z), axis=0)
    grads_near = jnp.concatenate(gather_y(grads_z), axis=0)
    weights = jnp.concatenate([gate_weight, up_weight], axis=1)
    weights_far = other_core(weights)
    down_far = other_core(down_weight)

    gate_up = (product(tokens_near, weights) + product(tokens_far, weights_far)).astype(BF)
    grads_far = after(grads_far, gate_up)
    gate_up = exchange(gate_up, "x")
    hidden_partial = (product_right_t(grads_near, down_weight) + product_right_t(grads_far, down_far)).astype(BF)
    both_weights = jnp.concatenate([weights, weights_far], axis=0)
    down_weights = jnp.concatenate([down_weight, down_far], axis=1)
    gate_up, hidden_partial, both_weights, down_weights = lax.optimization_barrier(
        (gate_up, hidden_partial, both_weights, down_weights)
    )
    gate_up = sum_parts(gate_up, X)
    gate_value = gate_up[:, :width]
    up_value = gate_up[:, width:]
    sigmoid_gate = jax.nn.sigmoid(gate_value)
    silu_gate = gate_value * sigmoid_gate
    hidden_share = (silu_gate * up_value).astype(BF)

    share = hidden_share.shape[0]
    mixed = jnp.concatenate(
        [jnp.broadcast_to(hidden_share[None], (X, share, width)), hidden_partial.reshape(X, share, width)], axis=1
    )
    mixed = exchange(mixed.reshape(2 * X * share, width), "x").reshape(X, 2 * share, width)
    mixed, tokens_moved, grads_moved = lax.optimization_barrier((mixed, other_core(tokens_far), other_core(grads_far)))
    hidden_half = mixed[:, :share].reshape(X * share, width)
    hidden_grad = jnp.sum(mixed[:, share:].astype(F32), axis=0)
    gate_grad = (hidden_grad * up_value * sigmoid_gate * (1.0 + gate_value * (1.0 - sigmoid_gate))).astype(BF)
    up_grad = (hidden_grad * silu_gate).astype(BF)
    grads_share = jnp.concatenate([gate_grad, up_grad], axis=1)
    grads_both = gather(grads_share, "x")

    hidden_half = after(hidden_half, grads_share)
    output_pieces = split_y(product(hidden_half, down_weights).astype(BF))
    output_moved = move_y(output_pieces)
    grads_both, *output_moved = lax.optimization_barrier((grads_both, *output_moved))
    input_pieces = split_y(product_right_t(grads_both, both_weights).astype(BF))
    input_moved = move_y(input_pieces)

    both_moved = other_core(after(grads_both, *input_pieces))
    hidden_moved = other_core(after(hidden_half, *input_pieces))
    output_total = reduce_z(after(sum_y(output_pieces[0], output_moved), both_moved))

    def over_tokens(left_halves, right_halves):
        return product_left_t(left_halves[0], right_halves[0]) + product_left_t(left_halves[1], right_halves[1])

    all_tokens = (tokens_near, tokens_moved)
    weight_grads = [
        over_tokens(all_tokens, (grads_both[:, :width], both_moved[:, :width])),
        over_tokens(all_tokens, (grads_both[:, width:], both_moved[:, width:])),
        over_tokens((hidden_half, hidden_moved), (grads_near, grads_moved)),
    ]
    input_moved, weight_grads, output_total = lax.optimization_barrier((input_moved, weight_grads, output_total))
    input_total = sum_y(input_pieces[0], input_moved)
    return (*own_columns((output_total, reduce_z(input_total)), first), *weight_grads)


def solution(mesh):
    grid = Mesh(mesh.devices.reshape(X, CORE, Y, Z), ("x", "core", "y", "z"))
    row, col = ("x", "core"), ("y", "z")
    in_specs = (P(col, row), P(row, col), P(row, col), P(col, row), P(col, row))
    out_specs = (P(col, row), P(col, row), P(row, col), P(row, col), P(col, row))
    return jax.shard_map(body, mesh=grid, in_specs=in_specs, out_specs=out_specs, check_vma=False)
```

```python
import jax
import jax.numpy as jnp
from jax import lax
from jax.sharding import Mesh, PartitionSpec as P

BF = jnp.bfloat16
F32 = jnp.float32
X, CORE, Y, Z = 4, 2, 4, 8


def product(left_side, right_side):
    return jnp.dot(left_side, right_side, preferred_element_type=F32)


def product_right_t(left_side, right_side):
    return lax.dot_general(left_side, right_side, (((1,), (1,)), ((), ())), preferred_element_type=F32)


def product_left_t(left_side, right_side):
    return lax.dot_general(left_side, right_side, (((0,), (0,)), ((), ())), preferred_element_type=F32)


def shift(block, axis, step):
    size = lax.axis_size(axis)
    return lax.ppermute(block, axis, [(i, (i + step) % size) for i in range(size)])


def exchange(blocks, axis):
    return lax.all_to_all(blocks, axis, split_axis=0, concat_axis=0, tiled=True)


def gather(block, axis):
    count = lax.axis_size(axis)
    rows, width = block.shape
    copies = jnp.broadcast_to(block[None], (count, rows, width)).reshape(count * rows, width)
    return exchange(copies, axis)


def after(block, *earlier):
    return lax.optimization_barrier((block,) + earlier)[0]


def swap_core(low, high):
    first = lax.axis_index("core") == 0
    return jnp.where(first, low, high), shift(jnp.where(first, high, low), "core", 1)


def sum_parts(parts, count):
    rows = parts.shape[0] // count
    return jnp.sum(parts.reshape((count, rows) + parts.shape[1:]).astype(F32), axis=0)


def reduce_core(partial):
    rows = partial.shape[0] // CORE
    kept, received = swap_core(partial[:rows], partial[rows:])
    return (kept.astype(F32) + received.astype(F32)).astype(BF)


def reduce_x(partial):
    return sum_parts(exchange(partial, "x"), X)


def gather_core(half):
    other = shift(half, "core", 1)
    first = lax.axis_index("core") == 0
    return jnp.concatenate([jnp.where(first, half, other), jnp.where(first, other, half)], axis=0)


def sum_y(own, moved):
    total = own.astype(F32)
    for piece in moved:
        total = total + piece.astype(F32)
    return total.astype(BF)


def reduce_z(total):
    return sum_parts(exchange(total, "z"), Z).astype(BF)


def order_tokens(own, left, right, far):
    rows = own.shape[0] // (CORE * X)
    width = own.shape[1]
    near = jnp.stack([left, right]).reshape(CORE, X, 2 * rows, width)
    parts = [own.reshape(CORE, X, rows, width), near, far.reshape(CORE, X, rows, width)]
    return jnp.concatenate(parts, axis=2).reshape(-1, width)


def split_tokens(block):
    width = block.shape[1]
    rows = block.shape[0] // (CORE * X * Y)
    parts = block.reshape(CORE, X, Y * rows, width)
    own, far = parts[:, :, :rows], parts[:, :, 3 * rows :]
    left, right = parts[0, :, rows : 3 * rows], parts[1, :, rows : 3 * rows]
    return [piece.reshape(-1, width) for piece in (own, left, right, far)]


def add(left_side, right_side):
    return (left_side.astype(F32) + right_side.astype(F32)).astype(BF)


def move_y_far(pieces):
    half = pieces[3].shape[0] // 2
    return shift(pieces[3][:half], "y", 1), shift(pieces[3][half:], "y", 3)


def add_y_far(pieces, from_left, from_right):
    half = pieces[3].shape[0] // 2
    to_right = jnp.concatenate([add(pieces[2][:half], from_left), pieces[2][half:]], axis=0)
    to_left = jnp.concatenate([pieces[1][:half], add(pieces[1][half:], from_right)], axis=0)
    return to_right, to_left


def move_y(pieces):
    return shift(pieces[1], "y", 3), shift(pieces[2], "y", 1), shift(pieces[3], "y", 2)


def body(tokens, gate_weight, up_weight, down_weight, out_grad):
    width = gate_weight.shape[1]
    both_weights = jnp.concatenate([gate_weight, up_weight], axis=1)

    tokens_z = gather(tokens, "z")
    grads_y = jnp.stack([out_grad, shift(out_grad, "y", 1), shift(out_grad, "y", 3), shift(out_grad, "y", 2)])
    tokens_z, grads_y, both_weights = lax.optimization_barrier((tokens_z, grads_y, both_weights))
    grads_all = lax.all_gather(grads_y, "z", axis=0, tiled=False)
    left, right = shift(tokens_z, "y", 1), shift(tokens_z, "y", 3)
    half = left.shape[0] // 2
    far = [shift(left[:half], "y", 1), shift(right[half:], "y", 3)]

    def pair_of(chunk):
        return reduce_core(product(chunk, both_weights).astype(BF))

    own_part = exchange(pair_of(tokens_z), "x")
    left, right, own_part = lax.optimization_barrier((left, right, own_part))
    near_part = exchange(pair_of(jnp.concatenate([left, right], axis=0)), "x")
    far, near_part = lax.optimization_barrier((far, near_part))
    far = jnp.concatenate(far, axis=0)
    far_part = exchange(pair_of(far), "x")
    gate_up = jnp.concatenate([sum_parts(part, X) for part in (own_part, near_part, far_part)], axis=0)
    gate_value = gate_up[:, :width]
    up_value = gate_up[:, width:]
    sigmoid_gate = jax.nn.sigmoid(gate_value)
    silu_gate = gate_value * sigmoid_gate
    hidden_half = gather((silu_gate * up_value).astype(BF), "x")

    grads_all = after(grads_all, far_part)
    grads_all = [grads_all[:, j].reshape(tokens_z.shape) for j in range(Y)]
    all_grads = order_tokens(*grads_all)
    hidden_partial = reduce_core(product_right_t(all_grads, down_weight).astype(BF))
    hidden_half, hidden_partial = lax.optimization_barrier((hidden_half, hidden_partial))
    hidden_grad = exchange(hidden_partial, "x")
    hidden = gather_core(hidden_half)
    output_pieces = split_tokens(product(hidden, down_weight).astype(BF))
    output_far = move_y_far(output_pieces)
    hidden_grad, *output_far = lax.optimization_barrier((hidden_grad, *output_far))
    to_right, to_left = lax.optimization_barrier(add_y_far(output_pieces, *output_far))
    output_near = shift(to_right, "y", 1), shift(to_left, "y", 3)
    hidden_grad = sum_parts(hidden_grad, X)
    gate_grad = (hidden_grad * up_value * sigmoid_gate * (1.0 + gate_value * (1.0 - sigmoid_gate))).astype(BF)
    up_grad = (hidden_grad * silu_gate).astype(BF)
    grads_half = gather(jnp.concatenate([gate_grad, up_grad], axis=1), "x")
    all_tokens = order_tokens(tokens_z, left, right, far)
    down_weight_grad = product_left_t(hidden, all_grads)
    grads_half, all_tokens, down_weight_grad, *output_near = lax.optimization_barrier(
        (grads_half, all_tokens, down_weight_grad, *output_near)
    )
    both_grads = gather_core(grads_half)

    input_pieces = lax.optimization_barrier(split_tokens(product_right_t(both_grads, both_weights).astype(BF)))
    input_moved = move_y(input_pieces)
    output_total = reduce_z(sum_y(after(output_pieces[0], *input_pieces), output_near))
    gate_weight_grad = product_left_t(all_tokens, both_grads[:, :width])
    up_weight_grad = product_left_t(all_tokens, both_grads[:, width:])
    weight_grads = (gate_weight_grad, up_weight_grad, down_weight_grad)
    input_moved, weight_grads, output_total = lax.optimization_barrier((input_moved, weight_grads, output_total))
    input_total = reduce_z(sum_y(input_pieces[0], input_moved))
    return (output_total, input_total) + weight_grads


def solution(mesh):
    grid = Mesh(mesh.devices.reshape(X, CORE, Y, Z), ("x", "core", "y", "z"))
    row, col = ("x", "core"), ("y", "z")
    in_specs = (P(col, row), P(row, col), P(row, col), P(col, row), P(col, row))
    out_specs = (P(col, row), P(col, row), P(row, col), P(row, col), P(col, row))
    return jax.shard_map(body, mesh=grid, in_specs=in_specs, out_specs=out_specs, check_vma=False)
```

```python
import jax
import jax.numpy as jnp
from jax import lax
from jax.experimental.layout import Layout, with_layout_constraint
from jax.sharding import Mesh, PartitionSpec as P

BF = jnp.bfloat16
F32 = jnp.float32
X, CORE, Y, Z = 4, 2, 4, 8


def product(left_side, right_side):
    return jnp.dot(left_side, right_side, preferred_element_type=F32)


def product_right_t(left_side, right_side):
    return lax.dot_general(left_side, right_side, (((1,), (1,)), ((), ())), preferred_element_type=F32)


def product_left_t(left_side, right_side):
    return lax.dot_general(left_side, right_side, (((0,), (0,)), ((), ())), preferred_element_type=F32)


def shift(block, axis, step):
    size = lax.axis_size(axis)
    return lax.ppermute(block, axis, [(i, (i + step) % size) for i in range(size)])


def exchange(blocks, axis):
    return lax.all_to_all(blocks, axis, split_axis=0, concat_axis=0, tiled=True)


def gather(block, axis):
    count = lax.axis_size(axis)
    rows, width = block.shape
    copies = jnp.broadcast_to(block[None], (count, rows, width)).reshape(count * rows, width)
    return exchange(copies, axis)


def after(block, *earlier):
    return lax.optimization_barrier((block,) + earlier)[0]


def gather_y(own):
    near = [shift(own, "y", 1), shift(own, "y", 3)]
    return [own, near[0], shift(own, "y", 2), near[1]]


def swap_core(low, high):
    first = lax.axis_index("core") == 0
    return jnp.where(first, low, high), shift(jnp.where(first, high, low), "core", 1)


def sum_parts(parts, count):
    rows = parts.shape[0] // count
    return jnp.sum(parts.reshape((count, rows) + parts.shape[1:]).astype(F32), axis=0)


def reduce_core(partial):
    rows = partial.shape[0] // CORE
    kept, received = swap_core(partial[:rows], partial[rows:])
    return (kept.astype(F32) + received.astype(F32)).astype(BF)


def reduce_x(partial):
    return sum_parts(exchange(partial, "x"), X)


def reduce_row(partial):
    rows = partial.shape[0] // CORE
    share = rows // X
    core, place = lax.axis_index("core"), lax.axis_index("x")
    received = shift(lax.dynamic_slice_in_dim(partial, (1 - core) * rows, rows, axis=0), "core", 1)

    def block(step):
        start = lax.bitwise_and(place + step, X - 1) * share
        kept = lax.dynamic_slice_in_dim(partial, core * rows + start, share, axis=0)
        return kept.astype(F32) + lax.dynamic_slice_in_dim(received, start, share, axis=0).astype(F32)

    sent = lax.optimization_barrier([block(step).astype(BF) for step in range(1, X)])
    moved = [shift(sent[step - 1], "x", step) for step in range(1, X)]
    total = block(0)
    for piece in moved:
        total = total + piece.astype(F32)
    return total


def gather_core(half):
    other = shift(half, "core", 1)
    first = lax.axis_index("core") == 0
    return jnp.concatenate([jnp.where(first, half, other), jnp.where(first, other, half)], axis=0)


def add(left_side, right_side):
    return (left_side.astype(F32) + right_side.astype(F32)).astype(BF)


def split_y(partial):
    rows = partial.shape[0] // Y
    return [partial[j * rows : (j + 1) * rows] for j in range(Y)]


def reduce_y_far(pieces):
    rows = pieces[2].shape[0] // 2
    return shift(pieces[2][:rows], "y", 1), shift(pieces[2][rows:], "y", 3)


def add_y_far(pieces, from_left, from_right):
    rows = pieces[2].shape[0] // 2
    to_right = jnp.concatenate([add(pieces[3][:rows], from_left), pieces[3][rows:]], axis=0)
    to_left = jnp.concatenate([pieces[1][:rows], add(pieces[1][rows:], from_right)], axis=0)
    return lax.optimization_barrier((to_right, to_left))


def move_y_near(to_right, to_left):
    return shift(to_right, "y", 1), shift(to_left, "y", 3)


def sum_y(own, from_left, from_right):
    return (own.astype(F32) + from_left.astype(F32) + from_right.astype(F32)).astype(BF)


def reduce_z(total):
    return sum_parts(exchange(total, "z"), Z).astype(BF)


def body(tokens, gate_weight, up_weight, down_weight, out_grad):
    width = gate_weight.shape[1]
    both_weights = jnp.concatenate([gate_weight, up_weight], axis=1)

    tokens_z = gather(tokens, "z")
    grads_y = jnp.stack(gather_y(out_grad))
    tokens_z, grads_y, both_weights = lax.optimization_barrier((tokens_z, grads_y, both_weights))
    all_tokens = jnp.concatenate(gather_y(tokens_z), axis=0)
    all_grads = lax.all_gather(grads_y, "z", axis=0, tiled=False)

    gate_up = with_layout_constraint(product(all_tokens, both_weights).astype(BF), Layout((0, 1)))
    gate_up = reduce_row(gate_up)
    all_grads = jnp.swapaxes(all_grads, 0, 1).reshape(all_tokens.shape)
    hidden_partial = reduce_core(product_right_t(all_grads, down_weight).astype(BF))
    gate_value = gate_up[:, :width]
    up_value = gate_up[:, width:]
    sigmoid_gate = jax.nn.sigmoid(gate_value)
    silu_gate = gate_value * sigmoid_gate
    hidden_share = (silu_gate * up_value).astype(BF)

    rows = hidden_share.shape[0]
    mixed = jnp.concatenate(
        [jnp.broadcast_to(hidden_share[None], (X, rows, width)), hidden_partial.reshape(X, rows, width)], axis=1
    )
    mixed = exchange(mixed.reshape(2 * X * rows, width), "x").reshape(X, 2 * rows, width)
    hidden = gather_core(mixed[:, :rows].reshape(X * rows, width))
    hidden_grad = jnp.sum(mixed[:, rows:].astype(F32), axis=0)

    output_pieces = split_y(product(hidden, down_weight).astype(BF))
    output_far = reduce_y_far(output_pieces)
    to_right, to_left = add_y_far(output_pieces, *output_far)
    output_near = move_y_near(to_right, to_left)

    gate_grad = (hidden_grad * up_value * sigmoid_gate * (1.0 + gate_value * (1.0 - sigmoid_gate))).astype(BF)
    up_grad = (hidden_grad * silu_gate).astype(BF)
    both_half = gather(jnp.concatenate([gate_grad, up_grad], axis=1), "x")
    down_weight_grad = product_left_t(hidden, all_grads)
    both_half, down_weight_grad, to_right, to_left = lax.optimization_barrier(
        (both_half, down_weight_grad, to_right, to_left)
    )
    both_grads = after(gather_core(both_half), *output_near)

    input_pieces = split_y(product_right_t(both_grads, both_weights).astype(BF))
    input_near = move_y_near(*add_y_far(input_pieces, *reduce_y_far(input_pieces)))
    output_total = reduce_z(sum_y(output_pieces[0], *output_near))
    weight_grads = (
        product_left_t(all_tokens, both_grads[:, :width]),
        product_left_t(all_tokens, both_grads[:, width:]),
        down_weight_grad,
    )
    input_near, weight_grads, output_total = lax.optimization_barrier((input_near, weight_grads, output_total))
    return (output_total, reduce_z(sum_y(input_pieces[0], *input_near))) + weight_grads


def solution(mesh):
    grid = Mesh(mesh.devices.reshape(X, CORE, Y, Z), ("x", "core", "y", "z"))
    row, col = ("x", "core"), ("y", "z")
    in_specs = (P(col, row), P(row, col), P(row, col), P(col, row), P(col, row))
    out_specs = (P(col, row), P(col, row), P(row, col), P(row, col), P(col, row))
    return jax.shard_map(body, mesh=grid, in_specs=in_specs, out_specs=out_specs, check_vma=False)
```

```python
import jax
import jax.numpy as jnp
from jax import lax
from jax.experimental.layout import Layout, with_layout_constraint
from jax.sharding import Mesh, PartitionSpec as P

BF = jnp.bfloat16
F32 = jnp.float32
X, CORE, Y, Z = 4, 2, 4, 8


def product(left_side, right_side):
    return jnp.dot(left_side, right_side, preferred_element_type=F32)


def product_right_t(left_side, right_side):
    return lax.dot_general(left_side, right_side, (((1,), (1,)), ((), ())), preferred_element_type=F32)


def product_left_t(left_side, right_side):
    return lax.dot_general(left_side, right_side, (((0,), (0,)), ((), ())), preferred_element_type=F32)


def shift(block, axis, step):
    size = lax.axis_size(axis)
    return lax.ppermute(block, axis, [(i, (i + step) % size) for i in range(size)])


def exchange(blocks, axis):
    return lax.all_to_all(blocks, axis, split_axis=0, concat_axis=0, tiled=True)


def gather(block, axis):
    count = lax.axis_size(axis)
    rows, width = block.shape
    copies = jnp.broadcast_to(block[None], (count, rows, width)).reshape(count * rows, width)
    return exchange(copies, axis)


def after(block, *earlier):
    return lax.optimization_barrier((block,) + earlier)[0]


def gather_y(own):
    near = [shift(own, "y", 1), shift(own, "y", 3)]
    return [own, near[0], shift(own, "y", 2), near[1]]


def swap_core(low, high):
    first = lax.axis_index("core") == 0
    return jnp.where(first, low, high), shift(jnp.where(first, high, low), "core", 1)


def sum_parts(parts, count):
    rows = parts.shape[0] // count
    return jnp.sum(parts.reshape((count, rows) + parts.shape[1:]).astype(F32), axis=0)


def reduce_core(partial):
    rows = partial.shape[0] // CORE
    kept, received = swap_core(partial[:rows], partial[rows:])
    return (kept.astype(F32) + received.astype(F32)).astype(BF)


def reduce_x(partial):
    return sum_parts(exchange(partial, "x"), X)


def reduce_row(partial):
    rows = partial.shape[0] // CORE
    share = rows // X
    core, place = lax.axis_index("core"), lax.axis_index("x")
    received = shift(lax.dynamic_slice_in_dim(partial, (1 - core) * rows, rows, axis=0), "core", 1)

    def block(step):
        start = lax.bitwise_and(place + step, X - 1) * share
        kept = lax.dynamic_slice_in_dim(partial, core * rows + start, share, axis=0)
        return kept.astype(F32) + lax.dynamic_slice_in_dim(received, start, share, axis=0).astype(F32)

    sent = lax.optimization_barrier([block(step).astype(BF) for step in range(1, X)])
    moved = [shift(sent[step - 1], "x", step) for step in range(1, X)]
    total = block(0)
    for piece in moved:
        total = total + piece.astype(F32)
    return total, sent


def gather_x(share):
    pieces = jnp.stack([share] + [shift(share, "x", step) for step in range(1, X)])
    place = lax.axis_index("x") + X
    return jnp.concatenate(
        [lax.dynamic_index_in_dim(pieces, lax.bitwise_and(place - i, X - 1), 0, keepdims=False) for i in range(X)], axis=0
    )


def gather_core(half):
    other = shift(half, "core", 1)
    first = lax.axis_index("core") == 0
    return jnp.concatenate([jnp.where(first, half, other), jnp.where(first, other, half)], axis=0)


def add(left_side, right_side):
    return (left_side.astype(F32) + right_side.astype(F32)).astype(BF)


def split_y(partial):
    rows = partial.shape[0] // Y
    return [partial[j * rows : (j + 1) * rows] for j in range(Y)]


def reduce_y_far(pieces):
    rows = pieces[2].shape[0] // 2
    return shift(pieces[2][:rows], "y", 1), shift(pieces[2][rows:], "y", 3)


def add_y_far(pieces, from_left, from_right):
    rows = pieces[2].shape[0] // 2
    to_right = jnp.concatenate([add(pieces[3][:rows], from_left), pieces[3][rows:]], axis=0)
    to_left = jnp.concatenate([pieces[1][:rows], add(pieces[1][rows:], from_right)], axis=0)
    return lax.optimization_barrier((to_right, to_left))


def move_y_near(to_right, to_left):
    return shift(to_right, "y", 1), shift(to_left, "y", 3)


def sum_y(own, from_left, from_right):
    return (own.astype(F32) + from_left.astype(F32) + from_right.astype(F32)).astype(BF)


def reduce_z(total):
    return sum_parts(exchange(total, "z"), Z).astype(BF)


def body(tokens, gate_weight, up_weight, down_weight, out_grad):
    width = gate_weight.shape[1]
    both_weights = jnp.concatenate([gate_weight, up_weight], axis=1)

    features = tokens.shape[1]
    main = features - features // 4
    tokens_z = gather(tokens[:, :main], "z")
    crossed = jnp.stack(gather_y(jnp.concatenate([out_grad, tokens[:, main:]], axis=1)))
    tokens_z, crossed, both_weights = lax.optimization_barrier((tokens_z, crossed, both_weights))
    all_grads = lax.all_gather(crossed[:, :, :features], "z", axis=0, tiled=False)
    rest = gather(crossed[:, :, features:].reshape(-1, features - main), "z")
    rest = jnp.swapaxes(rest.reshape(Z, Y, -1, features - main), 0, 1).reshape(-1, features - main)
    all_tokens = jnp.concatenate([jnp.concatenate(gather_y(tokens_z), axis=0), rest], axis=1)

    gate_up = with_layout_constraint(product(all_tokens, both_weights).astype(BF), Layout((0, 1)))
    gate_up, sent = reduce_row(gate_up)
    all_grads = after(all_grads, *sent)
    all_grads = jnp.swapaxes(all_grads, 0, 1).reshape(all_tokens.shape)
    hidden_partial = reduce_core(product_right_t(all_grads, down_weight).astype(BF))
    gate_value = gate_up[:, :width]
    up_value = gate_up[:, width:]
    sigmoid_gate = jax.nn.sigmoid(gate_value)
    silu_gate = gate_value * sigmoid_gate
    hidden_share = (silu_gate * up_value).astype(BF)

    hidden_half = gather_x(hidden_share)
    hidden_grad, hidden_half = lax.optimization_barrier((exchange(hidden_partial, "x"), hidden_half))
    hidden_grad = sum_parts(hidden_grad, X)
    hidden = gather_core(hidden_half)

    output_pieces = split_y(product(hidden, down_weight).astype(BF))
    output_far = reduce_y_far(output_pieces)
    to_right, to_left = add_y_far(output_pieces, *output_far)
    output_near = move_y_near(to_right, to_left)

    gate_grad = (hidden_grad * up_value * sigmoid_gate * (1.0 + gate_value * (1.0 - sigmoid_gate))).astype(BF)
    up_grad = (hidden_grad * silu_gate).astype(BF)
    both_half = gather(jnp.concatenate([gate_grad, up_grad], axis=1), "x")
    down_weight_grad = product_left_t(hidden, all_grads)
    both_half, down_weight_grad, to_right, to_left = lax.optimization_barrier(
        (both_half, down_weight_grad, to_right, to_left)
    )
    both_grads = after(gather_core(both_half), *output_near)

    input_pieces = split_y(product_right_t(both_grads, both_weights).astype(BF))
    input_near = move_y_near(*add_y_far(input_pieces, *reduce_y_far(input_pieces)))
    output_total = reduce_z(sum_y(output_pieces[0], *output_near))
    weight_grads = (
        product_left_t(all_tokens, both_grads[:, :width]),
        product_left_t(all_tokens, both_grads[:, width:]),
        down_weight_grad,
    )
    input_near, weight_grads, output_total = lax.optimization_barrier((input_near, weight_grads, output_total))
    return (output_total, reduce_z(sum_y(input_pieces[0], *input_near))) + weight_grads


def solution(mesh):
    grid = Mesh(mesh.devices.reshape(X, CORE, Y, Z), ("x", "core", "y", "z"))
    row, col = ("x", "core"), ("y", "z")
    in_specs = (P(col, row), P(row, col), P(row, col), P(col, row), P(col, row))
    out_specs = (P(col, row), P(col, row), P(row, col), P(row, col), P(col, row))
    return jax.shard_map(body, mesh=grid, in_specs=in_specs, out_specs=out_specs, check_vma=False)
```

```python
import jax
import jax.numpy as jnp
from jax import lax
from jax.experimental.layout import Layout, with_layout_constraint
from jax.sharding import Mesh, PartitionSpec as P

BF = jnp.bfloat16
F32 = jnp.float32
X, CORE, Y, Z = 4, 2, 4, 8


def product(left_side, right_side):
    return jnp.dot(left_side, right_side, preferred_element_type=F32)


def product_right_t(left_side, right_side):
    return lax.dot_general(left_side, right_side, (((1,), (1,)), ((), ())), preferred_element_type=F32)


def product_left_t(left_side, right_side):
    return lax.dot_general(left_side, right_side, (((0,), (0,)), ((), ())), preferred_element_type=F32)


def shift(block, axis, step):
    size = lax.axis_size(axis)
    return lax.ppermute(block, axis, [(i, (i + step) % size) for i in range(size)])


def exchange(blocks, axis):
    return lax.all_to_all(blocks, axis, split_axis=0, concat_axis=0, tiled=True)


def gather(block, axis):
    count = lax.axis_size(axis)
    rows, width = block.shape
    copies = jnp.broadcast_to(block[None], (count, rows, width)).reshape(count * rows, width)
    return exchange(copies, axis)


def after(block, *earlier):
    return lax.optimization_barrier((block,) + earlier)[0]


def gather_y(own):
    near = [shift(own, "y", 1), shift(own, "y", 3)]
    return [own, near[0], shift(own, "y", 2), near[1]]


def swap_core(low, high):
    first = lax.axis_index("core") == 0
    return jnp.where(first, low, high), shift(jnp.where(first, high, low), "core", 1)


def sum_parts(parts, count):
    rows = parts.shape[0] // count
    return jnp.sum(parts.reshape((count, rows) + parts.shape[1:]).astype(F32), axis=0)


def reduce_core(partial):
    rows = partial.shape[0] // CORE
    kept, received = swap_core(partial[:rows], partial[rows:])
    return (kept.astype(F32) + received.astype(F32)).astype(BF)


def reduce_x(partial):
    return sum_parts(exchange(partial, "x"), X)


def reduce_row(partial):
    rows = partial.shape[0] // CORE
    share = rows // X
    core, place = lax.axis_index("core"), lax.axis_index("x")
    received = shift(lax.dynamic_slice_in_dim(partial, (1 - core) * rows, rows, axis=0), "core", 1)

    def block(step):
        start = lax.bitwise_and(place + step, X - 1) * share
        kept = lax.dynamic_slice_in_dim(partial, core * rows + start, share, axis=0)
        return kept.astype(F32) + lax.dynamic_slice_in_dim(received, start, share, axis=0).astype(F32)

    sent = lax.optimization_barrier([block(step).astype(BF) for step in range(1, X)])
    moved = [shift(sent[step - 1], "x", step) for step in range(1, X)]
    total = block(0)
    for piece in moved:
        total = total + piece.astype(F32)
    return total, sent


def gather_x(share):
    pieces = jnp.stack([share] + [shift(share, "x", step) for step in range(1, X)])
    place = lax.axis_index("x") + X
    return jnp.concatenate(
        [lax.dynamic_index_in_dim(pieces, lax.bitwise_and(place - i, X - 1), 0, keepdims=False) for i in range(X)], axis=0
    )


def gather_core(half):
    other = shift(half, "core", 1)
    first = lax.axis_index("core") == 0
    return jnp.concatenate([jnp.where(first, half, other), jnp.where(first, other, half)], axis=0)


def add(left_side, right_side):
    return (left_side.astype(F32) + right_side.astype(F32)).astype(BF)


def split_y(partial):
    rows = partial.shape[0] // Y
    return [partial[j * rows : (j + 1) * rows] for j in range(Y)]


def reduce_y_far(pieces):
    rows = pieces[2].shape[0] // 2
    return shift(pieces[2][:rows], "y", 1), shift(pieces[2][rows:], "y", 3)


def add_y_far(pieces, from_left, from_right):
    rows = pieces[2].shape[0] // 2
    to_right = jnp.concatenate([add(pieces[3][:rows], from_left), pieces[3][rows:]], axis=0)
    to_left = jnp.concatenate([pieces[1][:rows], add(pieces[1][rows:], from_right)], axis=0)
    return lax.optimization_barrier((to_right, to_left))


def move_y_near(to_right, to_left):
    return shift(to_right, "y", 1), shift(to_left, "y", 3)


def sum_y(own, *moved):
    total = own.astype(F32)
    for piece in moved:
        total = total + piece.astype(F32)
    return total.astype(BF)


def reduce_z(total):
    return sum_parts(exchange(total, "z"), Z).astype(BF)


def body(tokens, gate_weight, up_weight, down_weight, out_grad):
    width = gate_weight.shape[1]
    both_weights = jnp.concatenate([gate_weight, up_weight], axis=1)

    tokens_z = gather(tokens, "z")
    grads_y = jnp.stack(gather_y(out_grad))
    tokens_z, grads_y, both_weights = lax.optimization_barrier((tokens_z, grads_y, both_weights))
    all_tokens = jnp.concatenate(gather_y(tokens_z), axis=0)
    all_grads = lax.all_gather(grads_y, "z", axis=0, tiled=False)

    gate_up = with_layout_constraint(product(all_tokens, both_weights).astype(BF), Layout((0, 1)))
    gate_up, sent = reduce_row(gate_up)
    all_grads = after(all_grads, *sent)
    all_grads = jnp.swapaxes(all_grads, 0, 1).reshape(all_tokens.shape)
    hidden_partial = reduce_core(product_right_t(all_grads, down_weight).astype(BF))
    gate_value = gate_up[:, :width]
    up_value = gate_up[:, width:]
    sigmoid_gate = jax.nn.sigmoid(gate_value)
    silu_gate = gate_value * sigmoid_gate
    hidden_share = (silu_gate * up_value).astype(BF)

    hidden_half = gather_x(hidden_share)
    hidden_grad, hidden_half = lax.optimization_barrier((exchange(hidden_partial, "x"), hidden_half))
    hidden_grad = sum_parts(hidden_grad, X)
    hidden = gather_core(hidden_half)

    output_pieces = split_y(product(hidden, down_weight).astype(BF))
    output_far = reduce_y_far(output_pieces)
    to_right, to_left = add_y_far(output_pieces, *output_far)
    output_near = move_y_near(to_right, to_left)

    gate_grad = (hidden_grad * up_value * sigmoid_gate * (1.0 + gate_value * (1.0 - sigmoid_gate))).astype(BF)
    up_grad = (hidden_grad * silu_gate).astype(BF)
    both_half = gather(jnp.concatenate([gate_grad, up_grad], axis=1), "x")
    both_half, to_right, to_left = lax.optimization_barrier((both_half, to_right, to_left))
    both_grads = after(gather_core(both_half), *output_near)

    input_pieces = lax.optimization_barrier(split_y(product_right_t(both_grads, both_weights).astype(BF)))
    input_moved = [shift(input_pieces[1], "y", 3), shift(input_pieces[3], "y", 1), shift(input_pieces[2], "y", 2)]
    down_weight_grad = product_left_t(after(hidden, *input_pieces), all_grads)
    gate_weight_grad = product_left_t(all_tokens, both_grads[:, :width])
    up_weight_grad = product_left_t(all_tokens, both_grads[:, width:])
    output_total = reduce_z(sum_y(after(output_pieces[0], *input_pieces), *output_near))
    input_moved, gate_weight_grad, up_weight_grad, down_weight_grad, output_total = lax.optimization_barrier(
        (input_moved, gate_weight_grad, up_weight_grad, down_weight_grad, output_total)
    )
    input_total = sum_y(input_pieces[0], *input_moved)
    return (output_total, reduce_z(input_total), gate_weight_grad, up_weight_grad, down_weight_grad)


def solution(mesh):
    grid = Mesh(mesh.devices.reshape(X, CORE, Y, Z), ("x", "core", "y", "z"))
    row, col = ("x", "core"), ("y", "z")
    in_specs = (P(col, row), P(row, col), P(row, col), P(col, row), P(col, row))
    out_specs = (P(col, row), P(col, row), P(row, col), P(row, col), P(col, row))
    return jax.shard_map(body, mesh=grid, in_specs=in_specs, out_specs=out_specs, check_vma=False)
```

```python
import jax
import jax.numpy as jnp
from jax import lax
from jax.experimental.layout import Layout, with_layout_constraint
from jax.sharding import Mesh, PartitionSpec as P

BF = jnp.bfloat16
F32 = jnp.float32
X, CORE, Y, Z = 4, 2, 4, 8


def product(left_side, right_side):
    return jnp.dot(left_side, right_side, preferred_element_type=F32)


def product_right_t(left_side, right_side):
    return lax.dot_general(left_side, right_side, (((1,), (1,)), ((), ())), preferred_element_type=F32)


def product_left_t(left_side, right_side):
    return lax.dot_general(left_side, right_side, (((0,), (0,)), ((), ())), preferred_element_type=F32)


def shift(block, axis, step):
    size = lax.axis_size(axis)
    return lax.ppermute(block, axis, [(i, (i + step) % size) for i in range(size)])


def exchange(blocks, axis):
    return lax.all_to_all(blocks, axis, split_axis=0, concat_axis=0, tiled=True)


def gather(block, axis):
    count = lax.axis_size(axis)
    rows, width = block.shape
    copies = jnp.broadcast_to(block[None], (count, rows, width)).reshape(count * rows, width)
    return exchange(copies, axis)


def after(block, *earlier):
    return lax.optimization_barrier((block,) + earlier)[0]


def gather_y(own):
    near = [shift(own, "y", 1), shift(own, "y", 3)]
    return [own, near[0], shift(own, "y", 2), near[1]]


def gather_y_halves(own):
    half = own.shape[0] // 2
    top, bottom = own[:half], own[half:]
    left_top, right_bottom = shift(top, "y", 1), shift(bottom, "y", 3)
    left_bottom, right_top = shift(bottom, "y", 1), shift(top, "y", 3)
    far_top, far_bottom = shift(left_top, "y", 1), shift(right_bottom, "y", 3)
    return [own, left_top, left_bottom, far_top, far_bottom, right_top, right_bottom]


def swap_core(low, high):
    first = lax.axis_index("core") == 0
    return jnp.where(first, low, high), shift(jnp.where(first, high, low), "core", 1)


def sum_parts(parts, count):
    rows = parts.shape[0] // count
    return jnp.sum(parts.reshape((count, rows) + parts.shape[1:]).astype(F32), axis=0)


def reduce_core(partial):
    rows = partial.shape[0] // CORE
    kept, received = swap_core(partial[:rows], partial[rows:])
    return (kept.astype(F32) + received.astype(F32)).astype(BF)


def reduce_x(partial):
    return sum_parts(exchange(partial, "x"), X)


def reduce_row(partial):
    rows = partial.shape[0] // CORE
    share = rows // X
    core, place = lax.axis_index("core"), lax.axis_index("x")
    received = shift(lax.dynamic_slice_in_dim(partial, (1 - core) * rows, rows, axis=0), "core", 1)

    def block(step):
        start = lax.bitwise_and(place + step, X - 1) * share
        kept = lax.dynamic_slice_in_dim(partial, core * rows + start, share, axis=0)
        return kept.astype(F32) + lax.dynamic_slice_in_dim(received, start, share, axis=0).astype(F32)

    sent = lax.optimization_barrier([block(step).astype(BF) for step in range(1, X)])
    moved = [shift(sent[step - 1], "x", step) for step in range(1, X)]
    total = block(0)
    for piece in moved:
        total = total + piece.astype(F32)
    return total, sent


def gather_x(share):
    pieces = jnp.stack([share] + [shift(share, "x", step) for step in range(1, X)])
    place = lax.axis_index("x") + X
    return jnp.concatenate(
        [lax.dynamic_index_in_dim(pieces, lax.bitwise_and(place - i, X - 1), 0, keepdims=False) for i in range(X)], axis=0
    )


def gather_core(half):
    other = shift(half, "core", 1)
    first = lax.axis_index("core") == 0
    return jnp.concatenate([jnp.where(first, half, other), jnp.where(first, other, half)], axis=0)


def add(left_side, right_side):
    return (left_side.astype(F32) + right_side.astype(F32)).astype(BF)


def split_y(partial):
    rows = partial.shape[0] // Y
    return [partial[j * rows : (j + 1) * rows] for j in range(Y)]


def move_y_first(pieces):
    half = pieces[2].shape[0] // 2
    to_right = jnp.concatenate([pieces[2][:half], pieces[3][half:]], axis=0)
    to_left = jnp.concatenate([pieces[2][half:], pieces[1][:half]], axis=0)
    return shift(to_right, "y", 1), shift(to_left, "y", 3)


def add_y_first(pieces, from_left, from_right):
    half = pieces[2].shape[0] // 2
    return lax.optimization_barrier(
        (add(pieces[3][:half], from_left[:half]), add(pieces[1][half:], from_right[:half]))
    )


def move_y_second(to_right, to_left):
    return shift(to_right, "y", 1), shift(to_left, "y", 3)


def sum_y_steps(own, first, second):
    half = own.shape[0] // 2
    top = sum_y(own[:half], second[0], first[1][half:])
    return jnp.concatenate([top, sum_y(own[half:], first[0][half:], second[1])], axis=0)


def sum_y(own, *moved):
    total = own.astype(F32)
    for piece in moved:
        total = total + piece.astype(F32)
    return total.astype(BF)


def reduce_z(total):
    return sum_parts(exchange(total, "z"), Z).astype(BF)


def body(tokens, gate_weight, up_weight, down_weight, out_grad):
    width = gate_weight.shape[1]
    both_weights = jnp.concatenate([gate_weight, up_weight], axis=1)

    tokens_z = gather(tokens, "z")
    grads_y = jnp.stack(gather_y(out_grad))
    tokens_z, grads_y, both_weights = lax.optimization_barrier((tokens_z, grads_y, both_weights))
    all_tokens = jnp.concatenate(gather_y_halves(tokens_z), axis=0)
    all_grads = lax.all_gather(grads_y, "z", axis=0, tiled=False)

    gate_up = with_layout_constraint(product(all_tokens, both_weights).astype(BF), Layout((0, 1)))
    gate_up, sent = reduce_row(gate_up)
    all_grads = after(all_grads, *sent)
    all_grads = jnp.swapaxes(all_grads, 0, 1).reshape(all_tokens.shape)
    hidden_partial = reduce_core(product_right_t(all_grads, down_weight).astype(BF))
    gate_value = gate_up[:, :width]
    up_value = gate_up[:, width:]
    sigmoid_gate = jax.nn.sigmoid(gate_value)
    silu_gate = gate_value * sigmoid_gate
    hidden_share = (silu_gate * up_value).astype(BF)

    hidden_half = gather_x(hidden_share)
    hidden_grad, hidden_half = lax.optimization_barrier((exchange(hidden_partial, "x"), hidden_half))
    hidden_grad = sum_parts(hidden_grad, X)
    hidden = gather_core(hidden_half)

    output_pieces = split_y(product(hidden, down_weight).astype(BF))
    output_first = move_y_first(output_pieces)
    to_right, to_left = add_y_first(output_pieces, *output_first)
    output_second = move_y_second(to_right, to_left)

    gate_grad = (hidden_grad * up_value * sigmoid_gate * (1.0 + gate_value * (1.0 - sigmoid_gate))).astype(BF)
    up_grad = (hidden_grad * silu_gate).astype(BF)
    both_half = gather(jnp.concatenate([gate_grad, up_grad], axis=1), "x")
    both_half, to_right, to_left = lax.optimization_barrier((both_half, to_right, to_left))
    both_grads = after(gather_core(both_half), *output_second)

    input_pieces = lax.optimization_barrier(split_y(product_right_t(both_grads, both_weights).astype(BF)))
    input_moved = [shift(input_pieces[1], "y", 3), shift(input_pieces[3], "y", 1), shift(input_pieces[2], "y", 2)]
    down_weight_grad = product_left_t(after(hidden, *input_pieces), all_grads)
    gate_weight_grad = product_left_t(all_tokens, both_grads[:, :width])
    up_weight_grad = product_left_t(all_tokens, both_grads[:, width:])
    output_total = reduce_z(sum_y_steps(after(output_pieces[0], *input_pieces), output_first, output_second))
    input_moved, gate_weight_grad, up_weight_grad, down_weight_grad, output_total = lax.optimization_barrier(
        (input_moved, gate_weight_grad, up_weight_grad, down_weight_grad, output_total)
    )
    input_total = sum_y(input_pieces[0], *input_moved)
    return (output_total, reduce_z(input_total), gate_weight_grad, up_weight_grad, down_weight_grad)


def solution(mesh):
    grid = Mesh(mesh.devices.reshape(X, CORE, Y, Z), ("x", "core", "y", "z"))
    row, col = ("x", "core"), ("y", "z")
    in_specs = (P(col, row), P(row, col), P(row, col), P(col, row), P(col, row))
    out_specs = (P(col, row), P(col, row), P(row, col), P(row, col), P(col, row))
    return jax.shard_map(body, mesh=grid, in_specs=in_specs, out_specs=out_specs, check_vma=False)
```

```python
import jax
import jax.numpy as jnp
from jax import lax
from jax.experimental.layout import Layout, with_layout_constraint
from jax.sharding import Mesh, PartitionSpec as P

BF = jnp.bfloat16
F32 = jnp.float32
X, CORE, Y, Z = 4, 2, 4, 8


def product(left_side, right_side):
    return jnp.dot(left_side, right_side, preferred_element_type=F32)


def product_right_t(left_side, right_side):
    return lax.dot_general(left_side, right_side, (((1,), (1,)), ((), ())), preferred_element_type=F32)


def product_left_t(left_side, right_side):
    return lax.dot_general(left_side, right_side, (((0,), (0,)), ((), ())), preferred_element_type=F32)


def shift(block, axis, step):
    size = lax.axis_size(axis)
    return lax.ppermute(block, axis, [(i, (i + step) % size) for i in range(size)])


def exchange(blocks, axis):
    return lax.all_to_all(blocks, axis, split_axis=0, concat_axis=0, tiled=True)


def gather(block, axis):
    count = lax.axis_size(axis)
    rows, width = block.shape
    copies = jnp.broadcast_to(block[None], (count, rows, width)).reshape(count * rows, width)
    return exchange(copies, axis)


def after(block, *earlier):
    return lax.optimization_barrier((block,) + earlier)[0]


def gather_y(own):
    near = [shift(own, "y", 1), shift(own, "y", 3)]
    return [own, near[0], shift(own, "y", 2), near[1]]


def gather_y_halves(own):
    half = own.shape[0] // 2
    top, bottom = own[:half], own[half:]
    left_top, right_bottom = shift(top, "y", 1), shift(bottom, "y", 3)
    left_bottom, right_top = shift(bottom, "y", 1), shift(top, "y", 3)
    far_top, far_bottom = shift(left_top, "y", 1), shift(right_bottom, "y", 3)
    return [own, left_top, left_bottom, far_top, far_bottom, right_top, right_bottom]


def swap_core(low, high):
    first = lax.axis_index("core") == 0
    return jnp.where(first, low, high), shift(jnp.where(first, high, low), "core", 1)


def sum_parts(parts, count):
    rows = parts.shape[0] // count
    return jnp.sum(parts.reshape((count, rows) + parts.shape[1:]).astype(F32), axis=0)


def reduce_core(partial):
    rows = partial.shape[0] // CORE
    kept, received = swap_core(partial[:rows], partial[rows:])
    return (kept.astype(F32) + received.astype(F32)).astype(BF)


def reduce_x(partial):
    return sum_parts(exchange(partial, "x"), X)


def reduce_row(partial):
    rows = partial.shape[0] // CORE
    share = rows // X
    core, place = lax.axis_index("core"), lax.axis_index("x")
    received = shift(lax.dynamic_slice_in_dim(partial, (1 - core) * rows, rows, axis=0), "core", 1)

    def block(step):
        start = lax.bitwise_and(place + step, X - 1) * share
        kept = lax.dynamic_slice_in_dim(partial, core * rows + start, share, axis=0)
        return kept.astype(F32) + lax.dynamic_slice_in_dim(received, start, share, axis=0).astype(F32)

    sent = lax.optimization_barrier([block(step).astype(BF) for step in range(1, X)])
    moved = [shift(sent[step - 1], "x", step) for step in range(1, X)]
    total = block(0)
    for piece in moved:
        total = total + piece.astype(F32)
    return total, sent


def gather_x(share):
    pieces = jnp.stack([share] + [shift(share, "x", step) for step in range(1, X)])
    place = lax.axis_index("x") + X
    return jnp.concatenate(
        [lax.dynamic_index_in_dim(pieces, lax.bitwise_and(place - i, X - 1), 0, keepdims=False) for i in range(X)], axis=0
    )


def gather_core(half):
    other = shift(half, "core", 1)
    first = lax.axis_index("core") == 0
    return jnp.concatenate([jnp.where(first, half, other), jnp.where(first, other, half)], axis=0)


def add(left_side, right_side):
    return (left_side.astype(F32) + right_side.astype(F32)).astype(BF)


def split_y(partial):
    rows = partial.shape[0] // Y
    return [partial[j * rows : (j + 1) * rows] for j in range(Y)]


def move_y_first(pieces):
    half = pieces[2].shape[0] // 2
    to_right = jnp.concatenate([pieces[2][:half], pieces[3][half:]], axis=0)
    to_left = jnp.concatenate([pieces[2][half:], pieces[1][:half]], axis=0)
    return shift(to_right, "y", 1), shift(to_left, "y", 3)


def add_y_first(pieces, from_left, from_right):
    half = pieces[2].shape[0] // 2
    return lax.optimization_barrier(
        (add(pieces[3][:half], from_left[:half]), add(pieces[1][half:], from_right[:half]))
    )


def move_y_second(to_right, to_left):
    return shift(to_right, "y", 1), shift(to_left, "y", 3)


def sum_y_steps(own, first, second):
    half = own.shape[0] // 2
    top = sum_y(own[:half], second[0], first[1][half:])
    return jnp.concatenate([top, sum_y(own[half:], first[0][half:], second[1])], axis=0)


def sum_y(own, *moved):
    total = own.astype(F32)
    for piece in moved:
        total = total + piece.astype(F32)
    return total.astype(BF)


def reduce_z(total):
    return sum_parts(exchange(total, "z"), Z).astype(BF)


def body(tokens, gate_weight, up_weight, down_weight, out_grad):
    width = gate_weight.shape[1]
    both_weights = jnp.concatenate([gate_weight, up_weight], axis=1)

    tokens_z = gather(tokens, "z")
    grads_y = jnp.stack(gather_y(out_grad))
    tokens_z = after(tokens_z, grads_y)
    all_tokens = jnp.concatenate(gather_y_halves(tokens_z), axis=0)
    all_grads = lax.all_gather(grads_y, "z", axis=0, tiled=False)

    gate_up = with_layout_constraint(product(all_tokens, both_weights).astype(BF), Layout((0, 1)))
    gate_up, sent = reduce_row(gate_up)
    all_grads = after(all_grads, *sent)
    all_grads = jnp.swapaxes(all_grads, 0, 1).reshape(all_tokens.shape)
    hidden_partial = reduce_core(product_right_t(all_grads, down_weight).astype(BF))
    gate_value = gate_up[:, :width]
    up_value = gate_up[:, width:]
    sigmoid_gate = jax.nn.sigmoid(gate_value)
    silu_gate = gate_value * sigmoid_gate
    hidden_share = (silu_gate * up_value).astype(BF)

    hidden_half = gather_x(hidden_share)
    hidden_grad, hidden_half = lax.optimization_barrier((exchange(hidden_partial, "x"), hidden_half))
    hidden_grad = sum_parts(hidden_grad, X)
    hidden = gather_core(hidden_half)

    output_pieces = split_y(product(hidden, down_weight).astype(BF))
    output_first = move_y_first(output_pieces)
    to_right, to_left = add_y_first(output_pieces, *output_first)
    output_second = move_y_second(to_right, to_left)

    gate_grad = (hidden_grad * up_value * sigmoid_gate * (1.0 + gate_value * (1.0 - sigmoid_gate))).astype(BF)
    up_grad = (hidden_grad * silu_gate).astype(BF)
    both_half = gather(jnp.concatenate([gate_grad, up_grad], axis=1), "x")
    both_half, to_right, to_left = lax.optimization_barrier((both_half, to_right, to_left))
    both_grads = after(gather_core(both_half), *output_second)

    input_pieces = lax.optimization_barrier(split_y(product_right_t(both_grads, both_weights).astype(BF)))
    input_moved = [shift(input_pieces[1], "y", 3), shift(input_pieces[3], "y", 1), shift(input_pieces[2], "y", 2)]
    down_weight_grad = product_left_t(after(hidden, *input_pieces), all_grads)
    gate_weight_grad = product_left_t(all_tokens, both_grads[:, :width])
    up_weight_grad = product_left_t(all_tokens, both_grads[:, width:])
    output_total = reduce_z(sum_y_steps(after(output_pieces[0], *input_pieces), output_first, output_second))
    input_moved, gate_weight_grad, up_weight_grad, down_weight_grad, output_total = lax.optimization_barrier(
        (input_moved, gate_weight_grad, up_weight_grad, down_weight_grad, output_total)
    )
    input_total = sum_y(input_pieces[0], *input_moved)
    return (output_total, reduce_z(input_total), gate_weight_grad, up_weight_grad, down_weight_grad)


def solution(mesh):
    grid = Mesh(mesh.devices.reshape(X, CORE, Y, Z), ("x", "core", "y", "z"))
    row, col = ("x", "core"), ("y", "z")
    in_specs = (P(col, row), P(row, col), P(row, col), P(col, row), P(col, row))
    out_specs = (P(col, row), P(col, row), P(row, col), P(row, col), P(col, row))
    return jax.shard_map(body, mesh=grid, in_specs=in_specs, out_specs=out_specs, check_vma=False)
```

```python
import jax
import jax.numpy as jnp
from jax import lax
from jax.experimental.layout import Layout, with_layout_constraint
from jax.sharding import Mesh, PartitionSpec as P

BF = jnp.bfloat16
F32 = jnp.float32
X, CORE, Y, Z = 4, 2, 4, 8


def product(left_side, right_side):
    return jnp.dot(left_side, right_side, preferred_element_type=F32)


def product_right_t(left_side, right_side):
    return lax.dot_general(left_side, right_side, (((1,), (1,)), ((), ())), preferred_element_type=F32)


def product_left_t(left_side, right_side):
    return lax.dot_general(left_side, right_side, (((0,), (0,)), ((), ())), preferred_element_type=F32)


def shift(block, axis, step):
    size = lax.axis_size(axis)
    return lax.ppermute(block, axis, [(i, (i + step) % size) for i in range(size)])


def exchange(blocks, axis):
    return lax.all_to_all(blocks, axis, split_axis=0, concat_axis=0, tiled=True)


def gather(block, axis):
    count = lax.axis_size(axis)
    rows, width = block.shape
    copies = jnp.broadcast_to(block[None], (count, rows, width)).reshape(count * rows, width)
    return exchange(copies, axis)


def after(block, *earlier):
    return lax.optimization_barrier((block,) + earlier)[0]


def gather_y(own):
    near = [shift(own, "y", 1), shift(own, "y", 3)]
    return [own, near[0], shift(own, "y", 2), near[1]]


def gather_y_halves(own):
    half = own.shape[0] // 2
    top, bottom = own[:half], own[half:]
    left_top, right_bottom = shift(top, "y", 1), shift(bottom, "y", 3)
    left_bottom, right_top = shift(bottom, "y", 1), shift(top, "y", 3)
    far_top, far_bottom = shift(left_top, "y", 1), shift(right_bottom, "y", 3)
    return [own, left_top, left_bottom, far_top, far_bottom, right_top, right_bottom]


def swap_core(low, high):
    first = lax.axis_index("core") == 0
    return jnp.where(first, low, high), shift(jnp.where(first, high, low), "core", 1)


def sum_parts(parts, count):
    rows = parts.shape[0] // count
    return jnp.sum(parts.reshape((count, rows) + parts.shape[1:]).astype(F32), axis=0)


def reduce_core(partial):
    rows = partial.shape[0] // CORE
    kept, received = swap_core(partial[:rows], partial[rows:])
    return (kept.astype(F32) + received.astype(F32)).astype(BF)


def reduce_x(partial):
    return sum_parts(exchange(partial, "x"), X)


def reduce_row(operand, weights):
    rows = operand.shape[0] // CORE
    share = rows // X
    core, place = lax.axis_index("core"), lax.axis_index("x")

    def half_of(index):
        part = product(lax.dynamic_slice_in_dim(operand, index * rows, rows, axis=0), weights).astype(BF)
        return with_layout_constraint(part, Layout((0, 1)))

    received = shift(half_of(1 - core), "core", 1)
    kept = half_of(core)

    def block(step):
        start = lax.bitwise_and(place + step, X - 1) * share
        return sum(lax.dynamic_slice_in_dim(part, start, share, axis=0).astype(F32) for part in (kept, received))

    sent = lax.optimization_barrier([block(step).astype(BF) for step in range(1, X)])
    moved = [shift(sent[step - 1], "x", step) for step in range(1, X)]
    total = block(0)
    for piece in moved:
        total = total + piece.astype(F32)
    return total, sent


def gather_x(share):
    pieces = jnp.stack([share] + [shift(share, "x", step) for step in range(1, X)])
    place = lax.axis_index("x") + X
    return jnp.concatenate(
        [lax.dynamic_index_in_dim(pieces, lax.bitwise_and(place - i, X - 1), 0, keepdims=False) for i in range(X)], axis=0
    )


def gather_core(half):
    other = shift(half, "core", 1)
    first = lax.axis_index("core") == 0
    return jnp.concatenate([jnp.where(first, half, other), jnp.where(first, other, half)], axis=0)


def add(left_side, right_side):
    return (left_side.astype(F32) + right_side.astype(F32)).astype(BF)


def split_y(partial):
    rows = partial.shape[0] // Y
    return [partial[j * rows : (j + 1) * rows] for j in range(Y)]


def first_rows(pieces):
    half = pieces[2].shape[0] // 2
    to_right = jnp.concatenate([pieces[2][:half], pieces[3][half:]], axis=0)
    to_left = jnp.concatenate([pieces[2][half:], pieces[1][:half]], axis=0)
    return to_right, to_left, pieces[3][:half], pieces[1][half:], pieces[0]


def add_y_first(to_right, to_left, from_left, from_right):
    half = to_right.shape[0]
    return lax.optimization_barrier((add(to_right, from_left[:half]), add(to_left, from_right[:half])))


def move_y_both(to_right, to_left):
    return shift(to_right, "y", 1), shift(to_left, "y", 3)


def sum_y_steps(own, first, second):
    half = own.shape[0] // 2
    top = sum_y(own[:half], second[0], first[1][half:])
    return jnp.concatenate([top, sum_y(own[half:], first[0][half:], second[1])], axis=0)


def sum_y(own, *moved):
    total = own.astype(F32)
    for piece in moved:
        total = total + piece.astype(F32)
    return total.astype(BF)


def reduce_z(total):
    return sum_parts(exchange(total, "z"), Z).astype(BF)


def body(tokens, gate_weight, up_weight, down_weight, out_grad):
    width = gate_weight.shape[1]
    both_weights = jnp.concatenate([gate_weight, up_weight], axis=1)

    tokens_z = gather(tokens, "z")
    grads_y = jnp.stack(gather_y(out_grad))
    tokens_z = after(tokens_z, grads_y)
    all_tokens = jnp.concatenate(gather_y_halves(tokens_z), axis=0)
    all_grads = lax.all_gather(grads_y, "z", axis=0, tiled=False)

    gate_up, sent = reduce_row(all_tokens, both_weights)
    all_grads = after(all_grads, *sent)
    all_grads = jnp.swapaxes(all_grads, 0, 1).reshape(all_tokens.shape)
    hidden_partial = reduce_core(product_right_t(all_grads, down_weight).astype(BF))
    gate_value = gate_up[:, :width]
    up_value = gate_up[:, width:]
    sigmoid_gate = jax.nn.sigmoid(gate_value)
    silu_gate = gate_value * sigmoid_gate
    hidden_share = (silu_gate * up_value).astype(BF)

    hidden_half = gather_x(hidden_share)
    hidden_grad, hidden_half = lax.optimization_barrier((exchange(hidden_partial, "x"), hidden_half))
    hidden_grad = sum_parts(hidden_grad, X)
    hidden = gather_core(hidden_half)

    output_rows = first_rows(split_y(hidden))
    output_parts = [product(part, down_weight).astype(BF) for part in output_rows[:4]]
    output_first = move_y_both(*output_parts[:2])
    to_right, to_left = add_y_first(*output_parts[2:4], *output_first)
    output_second = move_y_both(to_right, to_left)

    gate_grad = (hidden_grad * up_value * sigmoid_gate * (1.0 + gate_value * (1.0 - sigmoid_gate))).astype(BF)
    up_grad = (hidden_grad * silu_gate).astype(BF)
    both_half = gather(jnp.concatenate([gate_grad, up_grad], axis=1), "x")
    both_half, to_right, to_left = lax.optimization_barrier((both_half, to_right, to_left))
    both_grads = after(gather_core(both_half), *output_second)

    input_pieces = lax.optimization_barrier([product_right_t(part, both_weights).astype(BF) for part in split_y(both_grads)])
    input_moved = [shift(input_pieces[1], "y", 3), shift(input_pieces[3], "y", 1), shift(input_pieces[2], "y", 2)]
    down_weight_grad = product_left_t(after(hidden, *input_pieces), all_grads)
    later_grads = after(both_grads, *input_pieces)
    gate_weight_grad = product_left_t(all_tokens, later_grads[:, :width])
    up_weight_grad = product_left_t(all_tokens, later_grads[:, width:])
    output_total = reduce_z(sum_y_steps(product(after(output_rows[4], *input_pieces), down_weight).astype(BF), output_first, output_second))
    input_moved, gate_weight_grad, up_weight_grad, down_weight_grad, output_total = lax.optimization_barrier(
        (input_moved, gate_weight_grad, up_weight_grad, down_weight_grad, output_total)
    )
    input_total = sum_y(input_pieces[0], *input_moved)
    return (output_total, reduce_z(input_total), gate_weight_grad, up_weight_grad, down_weight_grad)


def solution(mesh):
    grid = Mesh(mesh.devices.reshape(X, CORE, Y, Z), ("x", "core", "y", "z"))
    row, col = ("x", "core"), ("y", "z")
    in_specs = (P(col, row), P(row, col), P(row, col), P(col, row), P(col, row))
    out_specs = (P(col, row), P(col, row), P(row, col), P(row, col), P(col, row))
    return jax.shard_map(body, mesh=grid, in_specs=in_specs, out_specs=out_specs, check_vma=False)
```

```python
import jax
import jax.numpy as jnp
from jax import lax
from jax.experimental.layout import Layout, with_layout_constraint
from jax.sharding import Mesh, PartitionSpec as P

BF = jnp.bfloat16
F32 = jnp.float32
X, CORE, Y, Z = 4, 2, 4, 8


def product(left_side, right_side):
    return jnp.dot(left_side, right_side, preferred_element_type=F32)


def product_right_t(left_side, right_side):
    return lax.dot_general(left_side, right_side, (((1,), (1,)), ((), ())), preferred_element_type=F32)


def product_left_t(left_side, right_side):
    return lax.dot_general(left_side, right_side, (((0,), (0,)), ((), ())), preferred_element_type=F32)


def shift(block, axis, step):
    size = lax.axis_size(axis)
    return lax.ppermute(block, axis, [(i, (i + step) % size) for i in range(size)])


def exchange(blocks, axis):
    return lax.all_to_all(blocks, axis, split_axis=0, concat_axis=0, tiled=True)


def gather(block, axis):
    count = lax.axis_size(axis)
    rows, width = block.shape
    copies = jnp.broadcast_to(block[None], (count, rows, width)).reshape(count * rows, width)
    return exchange(copies, axis)


def after(block, *earlier):
    return lax.optimization_barrier((block,) + earlier)[0]


def gather_y(own):
    near = [shift(own, "y", 1), shift(own, "y", 3)]
    return [own, near[0], shift(own, "y", 2), near[1]]


def gather_y_halves(own):
    half = own.shape[0] // 2
    top, bottom = own[:half], own[half:]
    left_top, right_bottom = shift(top, "y", 1), shift(bottom, "y", 3)
    left_bottom, right_top = shift(bottom, "y", 1), shift(top, "y", 3)
    far_top, far_bottom = shift(left_top, "y", 1), shift(right_bottom, "y", 3)
    return [own, left_top, left_bottom, far_top, far_bottom, right_top, right_bottom]


def swap_core(low, high):
    first = lax.axis_index("core") == 0
    return jnp.where(first, low, high), shift(jnp.where(first, high, low), "core", 1)


def sum_parts(parts, count):
    rows = parts.shape[0] // count
    return jnp.sum(parts.reshape((count, rows) + parts.shape[1:]).astype(F32), axis=0)


def reduce_core(partial):
    rows = partial.shape[0] // CORE
    kept, received = swap_core(partial[:rows], partial[rows:])
    return (kept.astype(F32) + received.astype(F32)).astype(BF)


def reduce_x(partial):
    return sum_parts(exchange(partial, "x"), X)


def reduce_row(partial):
    rows = partial.shape[0] // CORE
    share = rows // X
    core, place = lax.axis_index("core"), lax.axis_index("x")
    received = shift(lax.dynamic_slice_in_dim(partial, (1 - core) * rows, rows, axis=0), "core", 1)

    def block(step):
        start = lax.bitwise_and(place + step, X - 1) * share
        kept = lax.dynamic_slice_in_dim(partial, core * rows + start, share, axis=0)
        return kept.astype(F32) + lax.dynamic_slice_in_dim(received, start, share, axis=0).astype(F32)

    sent = lax.optimization_barrier([block(step).astype(BF) for step in range(1, X)])
    moved = [shift(sent[step - 1], "x", step) for step in range(1, X)]
    total = block(0)
    for piece in moved:
        total = total + piece.astype(F32)
    return total, sent


def gather_x(share):
    pieces = jnp.stack([share] + [shift(share, "x", step) for step in range(1, X)])
    place = lax.axis_index("x") + X
    return jnp.concatenate(
        [lax.dynamic_index_in_dim(pieces, lax.bitwise_and(place - i, X - 1), 0, keepdims=False) for i in range(X)], axis=0
    )


def gather_core(half):
    other = shift(half, "core", 1)
    first = lax.axis_index("core") == 0
    return jnp.concatenate([jnp.where(first, half, other), jnp.where(first, other, half)], axis=0)


def add(left_side, right_side):
    return (left_side.astype(F32) + right_side.astype(F32)).astype(BF)


def split_y(partial):
    rows = partial.shape[0] // Y
    return [partial[j * rows : (j + 1) * rows] for j in range(Y)]


def move_y_first(pieces):
    half = pieces[2].shape[0] // 2
    to_right = jnp.concatenate([pieces[2][:half], pieces[3][half:]], axis=0)
    to_left = jnp.concatenate([pieces[2][half:], pieces[1][:half]], axis=0)
    return shift(to_right, "y", 1), shift(to_left, "y", 3)


def add_y_first(pieces, from_left, from_right):
    half = pieces[2].shape[0] // 2
    return lax.optimization_barrier(
        (add(pieces[3][:half], from_left[:half]), add(pieces[1][half:], from_right[:half]))
    )


def move_y_second(to_right, to_left):
    return shift(to_right, "y", 1), shift(to_left, "y", 3)


def sum_y_steps(own, first, second):
    half = own.shape[0] // 2
    top = sum_y(own[:half], second[0], first[1][half:])
    return jnp.concatenate([top, sum_y(own[half:], first[0][half:], second[1])], axis=0)


def sum_y(own, *moved):
    total = own.astype(F32)
    for piece in moved:
        total = total + piece.astype(F32)
    return total.astype(BF)


def reduce_z(total):
    return sum_parts(exchange(total, "z"), Z).astype(BF)


def body(tokens, gate_weight, up_weight, down_weight, out_grad):
    width = gate_weight.shape[1]
    both_weights = jnp.concatenate([gate_weight, up_weight], axis=1)

    tokens_z = gather(tokens, "z")
    grads_y = jnp.stack(gather_y(out_grad))
    tokens_z = after(tokens_z, grads_y)
    all_tokens = jnp.concatenate(gather_y_halves(tokens_z), axis=0)
    all_grads = lax.all_gather(grads_y, "z", axis=0, tiled=False)

    gate_up = with_layout_constraint(product(all_tokens, both_weights).astype(BF), Layout((0, 1)))
    gate_up, sent = reduce_row(gate_up)
    all_grads = after(all_grads, *sent)
    hidden_partial = product_right_t(all_grads.reshape(all_tokens.shape), down_weight).astype(BF)
    hidden_partial = jnp.swapaxes(hidden_partial.reshape(all_grads.shape[:3] + (width,)), 0, 1).reshape(-1, width)
    hidden_partial = reduce_core(hidden_partial)
    all_grads = jnp.swapaxes(all_grads, 0, 1).reshape(all_tokens.shape)
    gate_value = gate_up[:, :width]
    up_value = gate_up[:, width:]
    sigmoid_gate = jax.nn.sigmoid(gate_value)
    silu_gate = gate_value * sigmoid_gate
    hidden_share = (silu_gate * up_value).astype(BF)

    hidden_half = gather_x(hidden_share)
    hidden_grad, hidden_half, all_grads = lax.optimization_barrier(
        (exchange(hidden_partial, "x"), hidden_half, all_grads)
    )
    hidden_grad = sum_parts(hidden_grad, X)
    hidden = gather_core(hidden_half)

    output_pieces = split_y(product(hidden, down_weight).astype(BF))
    output_first = move_y_first(output_pieces)
    to_right, to_left = add_y_first(output_pieces, *output_first)
    output_second = move_y_second(to_right, to_left)

    gate_grad = (hidden_grad * up_value * sigmoid_gate * (1.0 + gate_value * (1.0 - sigmoid_gate))).astype(BF)
    up_grad = (hidden_grad * silu_gate).astype(BF)
    both_half = gather(jnp.concatenate([gate_grad, up_grad], axis=1), "x")
    both_half, to_right, to_left = lax.optimization_barrier((both_half, to_right, to_left))
    both_grads = after(gather_core(both_half), *output_second)

    input_pieces = lax.optimization_barrier(split_y(product_right_t(both_grads, both_weights).astype(BF)))
    input_moved = [shift(input_pieces[1], "y", 3), shift(input_pieces[3], "y", 1), shift(input_pieces[2], "y", 2)]
    down_weight_grad = product_left_t(after(hidden, *input_pieces), all_grads)
    gate_weight_grad = product_left_t(all_tokens, both_grads[:, :width])
    up_weight_grad = product_left_t(all_tokens, both_grads[:, width:])
    output_total = reduce_z(sum_y_steps(after(output_pieces[0], *input_pieces), output_first, output_second))
    input_moved, gate_weight_grad, up_weight_grad, down_weight_grad, output_total = lax.optimization_barrier(
        (input_moved, gate_weight_grad, up_weight_grad, down_weight_grad, output_total)
    )
    input_total = sum_y(input_pieces[0], *input_moved)
    return (output_total, reduce_z(input_total), gate_weight_grad, up_weight_grad, down_weight_grad)


def solution(mesh):
    grid = Mesh(mesh.devices.reshape(X, CORE, Y, Z), ("x", "core", "y", "z"))
    row, col = ("x", "core"), ("y", "z")
    in_specs = (P(col, row), P(row, col), P(row, col), P(col, row), P(col, row))
    out_specs = (P(col, row), P(col, row), P(row, col), P(row, col), P(col, row))
    return jax.shard_map(body, mesh=grid, in_specs=in_specs, out_specs=out_specs, check_vma=False)
```
